256 devices in a mesh: row: 32 (over y, x, core), col: 8 (over z).
Axes of the slice: x: 4, y: 4, z: 8, core: 2. Of those that a mesh axis runs over, the one named last changes fastest.
Arguments:
- adjoint: float32 [4, 4, 4096, 1024], P(None, None, 'row', 'col'), may hold values from -24 to 24
- rate_scale: float32 [4, 4, 4096, 1024], P(None, None, 'row', 'col'), may hold values from 0.5 to 2
- kinetics: float32 [4, 4], replicated, may hold values from -3 to 3
- cross_matrix: float32 [4, 4], replicated, may hold values from -3 to 3
- x_diffusion: float32 [4, 4096], replicated, may hold values from 1 to 64
- y_diffusion: float32 [4, 1024], replicated, may hold values from 1 to 64
Outputs:
- adjoint_out: float32 [4, 4, 4096, 1024], P(None, None, 'row', 'col')
The draws below stay inside these ranges and needn't reach their ends.
All inputs are finite; a program needn't handle non-finite values.
Results may differ from the reference program's by a relative error of at most 0.0004.
Values sent between devices are 32-bit elements; how exact they have to be, the bound alone decides.
No kernel may reach another device: no remote copies, remote signals or barrier semaphores. Data moves between devices by JAX's collectives and lax.ppermute only.
A program may use at most 192 MiB of HBM per device.

```python
import math
import jax
import jax.numpy as jnp
from jax import lax

SPECIES = 4
NZ = 4
STEPS = 2
NX = 4096
NY = 1024


def level_of(rng, dims, cuts, smallest, largest):
    def one(axis_at, blocks):
        heights = jax.random.uniform(jax.random.fold_in(jax.random.fold_in(rng, 6), axis_at), (blocks,), jnp.float32, smallest / len(cuts), largest / len(cuts))
        return jnp.repeat(jnp.exp(heights), dims[axis_at] // blocks).reshape((-1,) + (1,) * (len(dims) - axis_at - 1))

    gain = one(*cuts[0])
    for cut in cuts[1:]:
        gain = gain * one(*cut)
    return gain


def normal_values(stream_key, shape, deviation, bound, split=(), kind=jnp.bfloat16):
    entries = jax.random.normal(stream_key, shape, jnp.float32) * deviation
    if len(split) > 0:
        entries = level_of(stream_key, shape, split, -0.22, 0.18) * entries
    return jnp.clip(entries, min=-bound, max=bound).astype(kind)


def setup_inputs(seed: int = 0) -> dict:
    key_of = jax.random.split(jax.random.key(seed), 7)
    adjoint = normal_values(key_of[0], (SPECIES, NZ, NX, NY), 4.0, 24.0, ((2, 32), (3, 8)), jnp.float32)
    rate_scale = jnp.clip(jnp.exp(math.log(2.0) - 1.3862944 * jax.random.uniform(key_of[1], (SPECIES, NZ, NX, NY), jnp.float32) ** level_of(key_of[1], (SPECIES, NZ, NX, NY), ((2, 32), (3, 8)), -0.2, 0.2)), 0.5, 2.0)
    kinetics = normal_values(key_of[2], (SPECIES, SPECIES), 0.5, 3.0, (), jnp.float32)
    cross_matrix = normal_values(key_of[3], (SPECIES, SPECIES), 0.5, 3.0, (), jnp.float32)
    x_diffusion = jnp.clip(jnp.exp(jax.random.uniform(key_of[4], (SPECIES, NX), jnp.float32, math.log(1.0), math.log(64.0))), 1.0, 64.0)
    y_diffusion = jnp.clip(jnp.exp(jax.random.uniform(key_of[5], (SPECIES, NY), jnp.float32, math.log(1.0), math.log(64.0))), 1.0, 64.0)
    return dict(adjoint=adjoint, rate_scale=rate_scale, kinetics=kinetics, cross_matrix=cross_matrix, x_diffusion=x_diffusion, y_diffusion=y_diffusion)


diffusion_number = 1000.0
react_step = 0.5
cross_step = 0.25
highest = lax.Precision.HIGHEST

def line_solve(values, kdiff):
    zero_fill = jnp.zeros_like(kdiff[:, :1])
    lower_band = -diffusion_number * jnp.concatenate([zero_fill, kdiff[:, :-1]], axis=1)
    main_band = 1.0 + 2.0 * diffusion_number * kdiff
    upper_band = -diffusion_number * jnp.concatenate([kdiff[:, 1:], zero_fill], axis=1)
    return lax.linalg.tridiagonal_solve(lower_band, main_band, upper_band, values)

def plane_steps(state, rate_plane, kinetics, cross_matrix, x_diffusion, y_diffusion):
    for repeat in range(STEPS):
        padded = jnp.pad(state, ((0, 0), (1, 1), (1, 1)))
        laplace = padded[:, 2:, 1:-1] + padded[:, :-2, 1:-1] + padded[:, 1:-1, 2:] + padded[:, 1:-1, :-2] - 4.0 * state
        reaction = rate_plane * jnp.einsum('ij,ixy->jxy', kinetics, state, precision=highest)
        mixing = jnp.einsum('ij,ixy->jxy', cross_matrix, laplace, precision=highest)
        explicit = state + react_step * reaction + cross_step * mixing
        xsolved = line_solve(explicit, x_diffusion)
        state = jnp.swapaxes(line_solve(jnp.swapaxes(xsolved, 1, 2), y_diffusion), 1, 2)
    return state

def reference(adjoint, rate_scale, kinetics, cross_matrix, x_diffusion, y_diffusion):

    def one_plane(planes):
        return plane_steps(planes[0], planes[1], kinetics, cross_matrix, x_diffusion, y_diffusion)
    result = lax.map(one_plane, (jnp.swapaxes(adjoint, 0, 1), jnp.swapaxes(rate_scale, 0, 1)))
    return jnp.swapaxes(result, 0, 1)
```

```python
import functools

import jax
import jax.numpy as jnp
from jax import lax
from jax.experimental import pallas as pl
from jax.experimental.pallas import tpu as pltpu
from jax.sharding import PartitionSpec as P

STEPS = 2
M = 1000.0
N = 128
EXT = N + 8
f32 = jnp.float32
bf16 = jnp.bfloat16
VMEM = 56 * 1024 * 1024


def iota(shape, dim):
    return lax.broadcasted_iota(jnp.int32, shape, dim)


def split(a):
    hi = a.astype(bf16)
    return hi, (a - hi.astype(f32)).astype(bf16)


def dot3(a, b, nt=False):
    dims = (((1,), (1 if nt else 0,)), ((), ()))
    ah, al = split(a)
    bh, bl = split(b)

    def dot(p, q):
        return lax.dot_general(p, q, dims, preferred_element_type=f32)

    return dot(ah, bh) + (dot(ah, bl) + dot(al, bh))


def tables_kernel(
    nx, ny, xd, yd, gx, lx, hx, gy, ry, hy, wx, wy,
    rows_x, rows_y, ex, ey, p0, p1, q0, q1,
):
    k = lax.axis_index("row")
    l = lax.axis_index("col")
    scale = 1.0 / M
    rows_x[...] = jnp.full((N, N), scale, f32)
    rows_y[...] = jnp.full((N, N), scale, f32)
    for j in range(nx):
        rows_x[4 * j : 4 * j + 4, :] = scale / xd[:, j * N : (j + 1) * N]
    for j in range(ny):
        rows_y[4 * j : 4 * j + 4, :] = scale / yd[:, j * N : (j + 1) * N]

    def block(ref, index):
        return scale / ref[:, pl.ds(pl.multiple_of(index * N, N), N)]

    rows_y[32:36, :] = block(xd, k)
    rows_y[36:40, :] = block(yd, l)
    rows_y[40:44, :] = block(xd, jnp.maximum(k - 1, 0)) * (k > 0).astype(f32)
    rows_y[44:48, :] = block(yd, jnp.maximum(l - 1, 0)) * (l > 0).astype(f32)
    rows_y[48:52, :] = block(xd, jnp.minimum(k + 1, nx - 1)) * (k < nx - 1).astype(f32)
    rows_y[52:56, :] = block(yd, jnp.minimum(l + 1, ny - 1)) * (l < ny - 1).astype(f32)
    ex[...] = rows_x[...].T
    ey[...] = rows_y[...].T

    first2 = (iota((2, N), 0) == 0).astype(f32)
    one, zero = jnp.ones((1, N), f32), jnp.zeros((1, N), f32)

    def body(i, carry):
        vx, dx, va, da, vb, db, ux, cx, ua, ca, ub, cb = carry
        at = pl.multiple_of(i * 8, 8)
        back = pl.multiple_of(N - 8 - i * 8, 8)
        ex_f, ey_f = ex[pl.ds(at, 8), :], ey[pl.ds(at, 8), :]
        ex_b, ey_b = ex[pl.ds(back, 8), :], ey[pl.ds(back, 8), :]
        for r in range(8):
            t = at + r
            p0[pl.ds(t, 1), :] = va
            p1[pl.ds(t, 1), :] = vb
            e, ee = ex_f[r : r + 1], ey_f[r : r + 1]
            dx = dx + e * vx
            vx = vx + dx
            da = da + ee * va
            va = va + da
            db = db + ee * vb
            vb = vb + db
            r2 = 7 - r
            t = back + r2
            q0[pl.ds(t, 1), :] = ua
            q1[pl.ds(t, 1), :] = ub
            e, ee = ex_b[r2 : r2 + 1], ey_b[r2 : r2 + 1]
            cx = cx + e * ux
            ux = ux + cx
            ca = ca + ee * ua
            ua = ua + ca
            cb = cb + ee * ub
            ub = ub + cb
        return vx, dx, va, da, vb, db, ux, cx, ua, ca, ub, cb

    init = (first2, 1.0 - first2, one, zero, zero, one)
    vx, dx, va, da, vb, db, ux, cx, ua, ca, ub, cb = lax.fori_loop(
        0, N // 8, body, init + init
    )

    row = iota((8, N), 0)
    lane = iota((8, N), 1)
    blk = lane // 4
    forward = row < 2
    is_x = row % 2 == 0
    count = jnp.where(is_x, nx, ny)
    own = jnp.where(is_x, k, l)
    place = jnp.where(forward, blk, count - 1 - blk)
    own = jnp.where(forward, own, count - 1 - own)

    def pack(a, b, c, d):
        return jnp.where(
            row == 0, a, jnp.where(row == 1, b, jnp.where(row == 2, c, d))
        )

    def shifted(a, by):
        return jnp.where(
            forward, pltpu.roll(a, 4 * by, 1), pltpu.roll(a, N - 4 * by, 1)
        )

    def outside(by):
        return place < by

    a0 = pack(vx[0:1], va, ux[0:1], ua)
    b0 = pack(vx[1:2], vb, ux[1:2], ub)
    c0 = pack(dx[0:1], da, cx[0:1], ca)
    d0 = pack(dx[1:2], db, cx[1:2], cb)
    a, b, c, d = a0, b0, c0, d0
    by = 1
    while by < max(nx, ny):
        skip = outside(by)
        sa = jnp.where(skip, 1.0, shifted(a, by))
        sb = jnp.where(skip, 0.0, shifted(b, by))
        sc = jnp.where(skip, 0.0, shifted(c, by))
        sd = jnp.where(skip, 1.0, shifted(d, by))
        a, b, c, d = a * sa + b * sc, a * sb + b * sd, c * sa + d * sc, c * sb + d * sd
        norm = 1.0 / (a + b)
        a, b, c, d = a * norm, b * norm, c * norm, d * norm
        by *= 2
    skip = outside(1)
    slope = jnp.where(skip, 1.0, shifted((c + d) / (a + b), 1))

    decay = (1.0 - slope) / ((a0 + b0 * slope) - (c0 + d0 * slope))
    between = (place < own) & (place >= 0)
    prod = jnp.where(between, decay, 1.0)

    def against(a, by):
        return jnp.where(
            forward, pltpu.roll(a, N - 4 * by, 1), pltpu.roll(a, 4 * by, 1)
        )

    def past(by):
        return place + by >= count

    by = 1
    while by < max(nx, ny):
        prod = prod * jnp.where(past(by), 1.0, against(prod, by))
        by *= 2
    weight = jnp.where(between, jnp.where(past(1), 1.0, against(prod, 1)), 0.0)

    def expand(width, per_block, species_of):
        src = iota((N, width), 0)
        col = iota((N, width), 1)
        hit = (src // 4 == col // per_block) & (src % 4 == species_of(col % per_block))
        return lax.dot_general(
            weight,
            jnp.where(hit, 1.0, 0.0),
            (((1,), (0,)), ((), ())),
            precision=lax.Precision.HIGHEST,
            preferred_element_type=f32,
        )

    width = nx * 16
    spread = expand(width, 16, lambda r: r // 4)
    rr, cc = iota((32, width), 0), iota((32, width), 1)
    wx[...] = jnp.where(
        rr % 16 == cc % 16, jnp.where(rr < 16, spread[0:1], spread[2:3]), 0.0
    )
    width = ny * 24
    spread = expand(width, 24, lambda r: jnp.where(r < 16, r // 4, r - 16))
    rr, cc = iota((40, width), 0), iota((40, width), 1)
    hit = jnp.where(rr < 32, rr % 16, 16 + rr % 4) == cc % 24
    left = (rr < 16) | ((rr >= 32) & (rr < 36))
    wy[...] = jnp.where(hit, jnp.where(left, spread[1:2], spread[3:4]), 0.0)

    lane1 = iota((1, N), 1)
    to_x = lax.rem(32 - 4 * k + N, N)
    to_y = lax.rem(36 - 4 * l + N, N)
    sx = pltpu.roll(slope, to_x, 1)
    sy = pltpu.roll(slope, to_y, 1)
    valid = (lane1 >= 32) & (lane1 < 40)
    sf = jnp.where(valid, jnp.where(lane1 < 36, sx[0:1], sy[1:2]), 1.0)
    sb = jnp.where(valid, jnp.where(lane1 < 36, sx[2:3], sy[3:4]), 1.0)
    phi = p0[...] + p1[...] * sf
    psi = q0[...] + q1[...] * sb
    phi_before, phi_after = 1.0 - sf, va + vb * sf
    psi_after, psi_before = 1.0 - sb, ua + ub * sb
    wron = sf * psi_before + (ca + cb * sb) * phi_before
    inv_w = 1.0 / wron
    psi = psi * inv_w
    psi_after, psi_before = psi_after * inv_w, psi_before * inv_w
    phi_t, psi_t = phi.T, psi.T
    eps = ey[...]
    eps_t = rows_y[...]
    i0, j0 = iota((N, N), 0), iota((N, N), 1)
    low = i0 >= j0
    r8 = iota((8, N), 0)
    c8 = iota((8, N), 1)
    for s in range(4):
        n = 32 + s
        e_b, e_a = eps_t[40 + s : 41 + s, N - 1 : N], eps_t[48 + s : 49 + s, 0:1]
        at = slice(n, n + 1)
        pr, qr = phi_t[at], psi_t[at]
        pc, qc, ec = phi[:, at], psi[:, at], eps[:, at]
        pb, pa, qb, qa = phi_before[:, at], phi_after[:, at], psi_before[:, at], psi_after[:, at]
        gx[s, 0:N, :] = jnp.where(low, (ec * qc) * pr, (ec * pc) * qr)
        gx[s, N:EXT, :] = jnp.where(
            r8 == 0, (e_b * pb) * qr, jnp.where(r8 == 1, (e_a * qa) * pr, 0.0)
        )
        lx[s, 0:N, :] = jnp.where(
            j0 == 0, ec * qc * pb, jnp.where(j0 == 1, ec * pc * qa, 0.0)
        )
        before = jnp.where(c8 == 0, e_b * pb * qb, e_b * pb * qa)
        after = jnp.where(c8 == 0, e_a * pb * qa, e_a * pa * qa)
        lx[s, N:EXT, :] = jnp.where(
            (r8 < 2) & (c8 < 2), jnp.where(r8 == 0, before, after), 0.0
        )
        hx[s] = jnp.where(
            r8 == 0, pr / pr[:, N - 1 : N], jnp.where(r8 == 1, qr / qr[:, 0:1], 0.0)
        )

        n = 36 + s
        e_b, e_a = eps_t[44 + s : 45 + s, N - 1 : N], eps_t[52 + s : 53 + s, 0:1]
        at = slice(n, n + 1)
        pr, qr, er = phi_t[at], psi_t[at], eps_t[at]
        pc, qc = phi[:, at], psi[:, at]
        pb, pa, qb, qa = phi_before[:, at], phi_after[:, at], psi_before[:, at], psi_after[:, at]
        gy[s, :, 0:N] = jnp.where(low, qc * (pr * er), pc * (qr * er))
        gy[s, :, N:] = jnp.where(
            j0 == 0, qc * (pb * e_b), jnp.where(j0 == 1, pc * (qa * e_a), 0.0)
        )
        ry[s, :, 0:N] = jnp.where(
            r8 == 0, pb * qr * er, jnp.where(r8 == 1, qa * pr * er, 0.0)
        )
        before = jnp.where(r8 == 0, e_b * pb * qb, e_b * pb * qa)
        after = jnp.where(r8 == 0, e_a * pb * qa, e_a * pa * qa)
        ry[s, :, N:] = jnp.where(
            (r8 < 2) & (c8 < 2), jnp.where(c8 == 0, before, after), 0.0
        )
        hy[s] = jnp.where(
            r8 == 0, pr / pr[:, N - 1 : N], jnp.where(r8 == 1, qr / qr[:, 0:1], 0.0)
        )


def edges_kernel(state, row_edges, col_edges):
    lane = iota((N, N), 1)
    cols = jnp.zeros((N, N), f32)
    for q in range(16):
        tile = state[q // 4, q % 4]
        row_edges[0, q : q + 1, :] = tile[0:1]
        row_edges[1, q : q + 1, :] = tile[N - 1 : N]
        cols = jnp.where(lane == q, tile[:, 0:1], cols)
        cols = jnp.where(lane == 16 + q, tile[:, N - 1 : N], cols)
    cols = cols.T
    col_edges[0] = cols[0:16]
    col_edges[1] = cols[16:32]


def explicit(tile_of, halo_of, rate, kin, cross, z, f_out):
    i0, j0 = iota((N, N), 0), iota((N, N), 1)
    tiles, laps = [], []
    for s in range(4):
        t = tile_of(s, z)
        up, down, left, right = halo_of(s, z)
        xm = jnp.where(i0 == 0, up, pltpu.roll(t, 1, 0))
        xp = jnp.where(i0 == N - 1, down, pltpu.roll(t, N - 1, 0))
        ym = jnp.where(j0 == 0, left, pltpu.roll(t, 1, 1))
        yp = jnp.where(j0 == N - 1, right, pltpu.roll(t, N - 1, 1))
        tiles.append(t)
        laps.append(xm + xp + ym + yp - 4.0 * t)
    for j in range(4):
        react = kin[0, j] * tiles[0]
        mix = cross[0, j] * laps[0]
        for i in range(1, 4):
            react = react + kin[i, j] * tiles[i]
            mix = mix + cross[i, j] * laps[i]
        f_out[j, :, z * N : (z + 1) * N] = (
            tiles[j] + 0.5 * rate[j, z] * react + 0.25 * mix
        )


def send_rows(f_out, hx, send, pay, nx):
    k = lax.axis_index("row")
    for s in range(4):
        ends = dot3(hx[s], f_out[s])
        for z in range(4):
            q = 4 * s + z
            pay[0, q : q + 1, :] = ends[0:1, z * N : (z + 1) * N]
            pay[1, q : q + 1, :] = ends[1:2, z * N : (z + 1) * N]
    a, b = pay[0], pay[1]
    for j in range(nx):
        send[j] = jnp.where(j > k, a, b)


def first_kernel(nx, state, rate, up, down, left, right, hx, kin, cross, f_out, send, cols, pay):
    zero = jnp.zeros((N - 32, N), f32)
    cols[...] = jnp.concatenate([left[...], right[...], zero], axis=0).T

    def halo_of(s, z):
        q = 4 * s + z
        return (
            up[q : q + 1, :],
            down[q : q + 1, :],
            cols[:, q : q + 1],
            cols[:, 16 + q : 17 + q],
        )

    for z in range(4):
        explicit(lambda s, z: state[s, z], halo_of, rate, kin, cross, z, f_out)
    send_rows(f_out, hx, send, pay, nx)


def rows_kernel(nx, ny, f_in, recv, wx, gx, lx, hy, g_out, send, pay):
    l = lax.axis_index("col")
    incoming = dot3(wx[...], recv[...].reshape(nx * 16, N))
    pay[...] = jnp.zeros_like(pay)
    for s in range(4):
        g = dot3(gx[s], f_in[s])
        lam, mu = lx[s, :, 0:1], lx[s, :, 1:2]
        parts, tails = [], []
        for z in range(4):
            q = 4 * s + z
            part = (
                g[:, z * N : (z + 1) * N]
                + lam * incoming[q : q + 1]
                + mu * incoming[16 + q : 17 + q]
            )
            g_out[s, z] = part
            parts.append(part[0:N])
            tails.append(part[N:EXT])
        ends = dot3(hy[s], jnp.concatenate(parts + tails, axis=0), nt=True)
        for p in range(2):
            for z in range(4):
                q = 4 * s + z
                pay[p, q : q + 1, :] = ends[p : p + 1, z * N : (z + 1) * N]
            pay[p, 16 + s : 17 + s, 0:32] = ends[p : p + 1, 4 * N : 4 * N + 32]
    a, b = pay[0], pay[1]
    for m in range(ny):
        send[m] = jnp.where(m > l, a, b)


def cols_part(ny, g_in, recv, wy, gy, ry, s, turned, wide):
    width = 2 * N if wide else N
    g = g_in[s].reshape(4 * EXT, N)
    out = dot3(g, gy[s, :, 0:width])
    lam, mu = ry[s, 0:1, 0:width], ry[s, 1:2, 0:width]
    result = []
    for z in range(4):
        q = 4 * s + z

        def column(p):
            main = turned[:, 16 * p + q : 16 * p + q + 1]
            tail = turned[8 * z : 8 * z + 8, 32 + 4 * p + s : 33 + 4 * p + s]
            return jnp.concatenate([main, tail], axis=0)

        result.append(
            out[z * EXT : (z + 1) * EXT] + column(0) * lam + column(1) * mu
        )
    return result


def turned_of(ny, recv, wy, turned):
    incoming = dot3(wy[...], recv[...].reshape(ny * 24, N))
    turned[...] = jnp.concatenate([incoming, jnp.zeros((N - 40, N), f32)], axis=0).T


def next_kernel(nx, ny, g_in, recv, wy, gy, ry, rate, hx, kin, cross, f_out, send, st, turned, pay):
    turned_of(ny, recv, wy, turned)
    for s in range(4):
        parts = cols_part(ny, g_in, recv, wy, gy, ry, s, turned, True)
        for z in range(4):
            st[s, z] = parts[z]

    def halo_of(s, z):
        return (
            st[s, z, N : N + 1, 0:N],
            st[s, z, N + 1 : N + 2, 0:N],
            st[s, z, 0:N, N : N + 1],
            st[s, z, 0:N, N + 1 : N + 2],
        )

    for z in range(4):
        explicit(lambda s, z: st[s, z, 0:N, 0:N], halo_of, rate, kin, cross, z, f_out)
    send_rows(f_out, hx, send, pay, nx)


def last_kernel(ny, g_in, recv, wy, gy, ry, out, turned):
    turned_of(ny, recv, wy, turned)
    for s in range(4):
        parts = cols_part(ny, g_in, recv, wy, gy, ry, s, turned, False)
        for z in range(4):
            out[s, z] = parts[z][0:N]


def call(body, outs, scratch, smem=0, cost=3_000_000):
    shapes = [jax.ShapeDtypeStruct(shape, f32) for shape in outs]

    def run(*args):
        count = len(args) - smem
        return pl.pallas_call(
            body,
            out_shape=shapes,
            in_specs=[pl.BlockSpec(memory_space=pltpu.VMEM)] * count
            + [pl.BlockSpec(memory_space=pltpu.SMEM)] * smem,
            out_specs=[pl.BlockSpec(memory_space=pltpu.VMEM)] * len(shapes),
            scratch_shapes=[pltpu.VMEM(shape, f32) for shape in scratch],
            compiler_params=pltpu.CompilerParams(vmem_limit_bytes=VMEM),
            cost_estimate=pl.CostEstimate(
                flops=cost * 1000, bytes_accessed=cost, transcendentals=0
            ),
        )(*args)

    return run


def on_device(adjoint, rate_scale, kinetics, cross_matrix, x_diffusion, y_diffusion):
    nx, ny = lax.axis_size("row"), lax.axis_size("col")
    row_edges, col_edges = call(edges_kernel, [(2, 16, N), (2, 16, N)], [])(adjoint)
    up = lax.ppermute(row_edges[1], "row", [(i, i + 1) for i in range(nx - 1)])
    down = lax.ppermute(row_edges[0], "row", [(i + 1, i) for i in range(nx - 1)])
    left = lax.ppermute(col_edges[1], "col", [(i, i + 1) for i in range(ny - 1)])
    right = lax.ppermute(col_edges[0], "col", [(i + 1, i) for i in range(ny - 1)])
    gx, lx, hx, gy, ry, hy, wx, wy = call(
        functools.partial(tables_kernel, nx, ny),
        [
            (4, EXT, N), (4, EXT, N), (4, 8, N), (4, N, 2 * N), (4, 8, 2 * N), (4, 8, N),
            (32, nx * 16), (40, ny * 24),
        ],
        [(N, N)] * 8,
    )(x_diffusion, y_diffusion)
    f_shape, g_shape = (4, N, 4 * N), (4, 4, EXT, N)
    send_x, send_y = (nx, 16, N), (ny, 24, N)
    f, send = call(
        functools.partial(first_kernel, nx), [f_shape, send_x], [(N, N), (2, 16, N)], 2
    )(adjoint, rate_scale, up, down, left, right, hx, kinetics, cross_matrix)
    for step in range(STEPS):
        recv = lax.all_to_all(send, "row", 0, 0, tiled=True)
        g, send = call(
            functools.partial(rows_kernel, nx, ny), [g_shape, send_y], [(2, 24, N)]
        )(f, recv, wx, gx, lx, hy)
        recv = lax.all_to_all(send, "col", 0, 0, tiled=True)
        if step + 1 < STEPS:
            f, send = call(
                functools.partial(next_kernel, nx, ny),
                [f_shape, send_x],
                [(4, 4, EXT, 2 * N), (N, N), (2, 16, N)],
                2,
            )(g, recv, wy, gy, ry, rate_scale, hx, kinetics, cross_matrix)
        else:
            (out,) = call(functools.partial(last_kernel, ny), [(4, 4, N, N)], [(N, N)])(
                g, recv, wy, gy, ry
            )
    return out


def solution(mesh):
    return jax.shard_map(
        on_device,
        mesh=mesh,
        in_specs=(P(None, None, "row", "col"), P(None, None, "row", "col"), P(), P(), P(), P()),
        out_specs=P(None, None, "row", "col"),
        check_vma=False,
    )
```

```python
import functools

import jax
import jax.numpy as jnp
from jax import lax
from jax.experimental import pallas as pl
from jax.experimental.pallas import tpu as pltpu
from jax.sharding import PartitionSpec as P

STEPS = 2
M = 1000.0
N = 128
EXT = N + 8
f32 = jnp.float32
bf16 = jnp.bfloat16
VMEM = 20 * 1024 * 1024


def iota(shape, dim):
    return lax.broadcasted_iota(jnp.int32, shape, dim)


def split(a):
    hi = a.astype(bf16)
    return hi, (a - hi.astype(f32)).astype(bf16)


def dot3(a, b, nt=False):
    dims = (((1,), (1 if nt else 0,)), ((), ()))
    ah, al = split(a)
    bh, bl = split(b)

    def dot(p, q):
        return lax.dot_general(p, q, dims, preferred_element_type=f32)

    return dot(ah, bh) + (dot(ah, bl) + dot(al, bh))


def tables_kernel(
    nx, ny, xd, yd, gx, lx, hx, gy, ry, hy, wx, wy,
    rows_x, rows_y, ex, ey, p0, p1, q0, q1,
):
    k = lax.axis_index("row")
    l = lax.axis_index("col")
    scale = 1.0 / M
    rows_x[...] = jnp.full((N, N), scale, f32)
    rows_y[...] = jnp.full((N, N), scale, f32)
    for j in range(nx):
        rows_x[4 * j : 4 * j + 4, :] = scale / xd[:, j * N : (j + 1) * N]
    for j in range(ny):
        rows_y[4 * j : 4 * j + 4, :] = scale / yd[:, j * N : (j + 1) * N]

    def block(ref, index):
        return scale / ref[:, pl.ds(pl.multiple_of(index * N, N), N)]

    rows_y[32:36, :] = block(xd, k)
    rows_y[36:40, :] = block(yd, l)
    rows_y[40:44, :] = block(xd, jnp.maximum(k - 1, 0)) * (k > 0).astype(f32)
    rows_y[44:48, :] = block(yd, jnp.maximum(l - 1, 0)) * (l > 0).astype(f32)
    rows_y[48:52, :] = block(xd, jnp.minimum(k + 1, nx - 1)) * (k < nx - 1).astype(f32)
    rows_y[52:56, :] = block(yd, jnp.minimum(l + 1, ny - 1)) * (l < ny - 1).astype(f32)
    ex[...] = rows_x[...].T
    ey[...] = rows_y[...].T

    first2 = (iota((2, N), 0) == 0).astype(f32)
    one, zero = jnp.ones((1, N), f32), jnp.zeros((1, N), f32)

    def body(i, carry):
        vx, dx, va, da, vb, db, ux, cx, ua, ca, ub, cb = carry
        at = pl.multiple_of(i * 8, 8)
        back = pl.multiple_of(N - 8 - i * 8, 8)
        ex_f, ey_f = ex[pl.ds(at, 8), :], ey[pl.ds(at, 8), :]
        ex_b, ey_b = ex[pl.ds(back, 8), :], ey[pl.ds(back, 8), :]
        for r in range(8):
            t = at + r
            p0[pl.ds(t, 1), :] = va
            p1[pl.ds(t, 1), :] = vb
            e, ee = ex_f[r : r + 1], ey_f[r : r + 1]
            dx = dx + e * vx
            vx = vx + dx
            da = da + ee * va
            va = va + da
            db = db + ee * vb
            vb = vb + db
            r2 = 7 - r
            t = back + r2
            q0[pl.ds(t, 1), :] = ua
            q1[pl.ds(t, 1), :] = ub
            e, ee = ex_b[r2 : r2 + 1], ey_b[r2 : r2 + 1]
            cx = cx + e * ux
            ux = ux + cx
            ca = ca + ee * ua
            ua = ua + ca
            cb = cb + ee * ub
            ub = ub + cb
        return vx, dx, va, da, vb, db, ux, cx, ua, ca, ub, cb

    init = (first2, 1.0 - first2, one, zero, zero, one)
    vx, dx, va, da, vb, db, ux, cx, ua, ca, ub, cb = lax.fori_loop(
        0, N // 8, body, init + init
    )

    row = iota((8, N), 0)
    lane = iota((8, N), 1)
    blk = lane // 4
    forward = row < 2
    is_x = row % 2 == 0
    count = jnp.where(is_x, nx, ny)
    own = jnp.where(is_x, k, l)
    place = jnp.where(forward, blk, count - 1 - blk)
    own = jnp.where(forward, own, count - 1 - own)

    def pack(a, b, c, d):
        return jnp.where(
            row == 0, a, jnp.where(row == 1, b, jnp.where(row == 2, c, d))
        )

    def shifted(a, by):
        return jnp.where(
            forward, pltpu.roll(a, 4 * by, 1), pltpu.roll(a, N - 4 * by, 1)
        )

    def outside(by):
        return place < by

    a0 = pack(vx[0:1], va, ux[0:1], ua)
    b0 = pack(vx[1:2], vb, ux[1:2], ub)
    c0 = pack(dx[0:1], da, cx[0:1], ca)
    d0 = pack(dx[1:2], db, cx[1:2], cb)
    a, b, c, d = a0, b0, c0, d0
    by = 1
    while by < max(nx, ny):
        skip = outside(by)
        sa = jnp.where(skip, 1.0, shifted(a, by))
        sb = jnp.where(skip, 0.0, shifted(b, by))
        sc = jnp.where(skip, 0.0, shifted(c, by))
        sd = jnp.where(skip, 1.0, shifted(d, by))
        a, b, c, d = a * sa + b * sc, a * sb + b * sd, c * sa + d * sc, c * sb + d * sd
        norm = 1.0 / (a + b)
        a, b, c, d = a * norm, b * norm, c * norm, d * norm
        by *= 2
    skip = outside(1)
    slope = jnp.where(skip, 1.0, shifted((c + d) / (a + b), 1))

    decay = (1.0 - slope) / ((a0 + b0 * slope) - (c0 + d0 * slope))
    between = (place < own) & (place >= 0)
    prod = jnp.where(between, decay, 1.0)

    def against(a, by):
        return jnp.where(
            forward, pltpu.roll(a, N - 4 * by, 1), pltpu.roll(a, 4 * by, 1)
        )

    def past(by):
        return place + by >= count

    by = 1
    while by < max(nx, ny):
        prod = prod * jnp.where(past(by), 1.0, against(prod, by))
        by *= 2
    weight = jnp.where(between, jnp.where(past(1), 1.0, against(prod, 1)), 0.0)

    def expand(width, per_block, species_of):
        src = iota((N, width), 0)
        col = iota((N, width), 1)
        hit = (src // 4 == col // per_block) & (src % 4 == species_of(col % per_block))
        return lax.dot_general(
            weight,
            jnp.where(hit, 1.0, 0.0),
            (((1,), (0,)), ((), ())),
            precision=lax.Precision.HIGHEST,
            preferred_element_type=f32,
        )

    width = nx * 16
    spread = expand(width, 16, lambda r: r // 4)
    rr, cc = iota((32, width), 0), iota((32, width), 1)
    wx[...] = jnp.where(
        rr % 16 == cc % 16, jnp.where(rr < 16, spread[0:1], spread[2:3]), 0.0
    )
    width = ny * 24
    spread = expand(width, 24, lambda r: jnp.where(r < 16, r // 4, r - 16))
    rr, cc = iota((40, width), 0), iota((40, width), 1)
    hit = jnp.where(rr < 32, rr % 16, 16 + rr % 4) == cc % 24
    left = (rr < 16) | ((rr >= 32) & (rr < 36))
    wy[...] = jnp.where(hit, jnp.where(left, spread[1:2], spread[3:4]), 0.0)

    lane1 = iota((1, N), 1)
    to_x = lax.rem(32 - 4 * k + N, N)
    to_y = lax.rem(36 - 4 * l + N, N)
    sx = pltpu.roll(slope, to_x, 1)
    sy = pltpu.roll(slope, to_y, 1)
    valid = (lane1 >= 32) & (lane1 < 40)
    sf = jnp.where(valid, jnp.where(lane1 < 36, sx[0:1], sy[1:2]), 1.0)
    sb = jnp.where(valid, jnp.where(lane1 < 36, sx[2:3], sy[3:4]), 1.0)
    phi = p0[...] + p1[...] * sf
    psi = q0[...] + q1[...] * sb
    phi_before, phi_after = 1.0 - sf, va + vb * sf
    psi_after, psi_before = 1.0 - sb, ua + ub * sb
    wron = sf * psi_before + (ca + cb * sb) * phi_before
    inv_w = 1.0 / wron
    psi = psi * inv_w
    psi_after, psi_before = psi_after * inv_w, psi_before * inv_w
    phi_t, psi_t = phi.T, psi.T
    eps = ey[...]
    eps_t = rows_y[...]
    i0, j0 = iota((N, N), 0), iota((N, N), 1)
    low = i0 >= j0
    r8 = iota((8, N), 0)
    c8 = iota((8, N), 1)
    for s in range(4):
        n = 32 + s
        e_b, e_a = eps_t[40 + s : 41 + s, N - 1 : N], eps_t[48 + s : 49 + s, 0:1]
        at = slice(n, n + 1)
        pr, qr = phi_t[at], psi_t[at]
        pc, qc, ec = phi[:, at], psi[:, at], eps[:, at]
        pb, pa, qb, qa = phi_before[:, at], phi_after[:, at], psi_before[:, at], psi_after[:, at]
        gx[s, 0:N, :] = jnp.where(low, (ec * qc) * pr, (ec * pc) * qr)
        gx[s, N:EXT, :] = jnp.where(
            r8 == 0, (e_b * pb) * qr, jnp.where(r8 == 1, (e_a * qa) * pr, 0.0)
        )
        lx[s, 0:N, :] = jnp.where(
            j0 == 0, ec * qc * pb, jnp.where(j0 == 1, ec * pc * qa, 0.0)
        )
        before = jnp.where(c8 == 0, e_b * pb * qb, e_b * pb * qa)
        after = jnp.where(c8 == 0, e_a * pb * qa, e_a * pa * qa)
        lx[s, N:EXT, :] = jnp.where(
            (r8 < 2) & (c8 < 2), jnp.where(r8 == 0, before, after), 0.0
        )
        hx[s] = jnp.where(
            r8 == 0, pr / pr[:, N - 1 : N], jnp.where(r8 == 1, qr / qr[:, 0:1], 0.0)
        )

        n = 36 + s
        e_b, e_a = eps_t[44 + s : 45 + s, N - 1 : N], eps_t[52 + s : 53 + s, 0:1]
        at = slice(n, n + 1)
        pr, qr, er = phi_t[at], psi_t[at], eps_t[at]
        pc, qc = phi[:, at], psi[:, at]
        pb, pa, qb, qa = phi_before[:, at], phi_after[:, at], psi_before[:, at], psi_after[:, at]
        gy[s, :, 0:N] = jnp.where(low, qc * (pr * er), pc * (qr * er))
        gy[s, :, N:] = jnp.where(
            j0 == 0, qc * (pb * e_b), jnp.where(j0 == 1, pc * (qa * e_a), 0.0)
        )
        ry[s, :, 0:N] = jnp.where(
            r8 == 0, pb * qr * er, jnp.where(r8 == 1, qa * pr * er, 0.0)
        )
        before = jnp.where(r8 == 0, e_b * pb * qb, e_b * pb * qa)
        after = jnp.where(r8 == 0, e_a * pb * qa, e_a * pa * qa)
        ry[s, :, N:] = jnp.where(
            (r8 < 2) & (c8 < 2), jnp.where(c8 == 0, before, after), 0.0
        )
        hy[s] = jnp.where(
            r8 == 0, pr / pr[:, N - 1 : N], jnp.where(r8 == 1, qr / qr[:, 0:1], 0.0)
        )


def edges_kernel(state, row_edges, col_edges):
    lane = iota((N, N), 1)
    cols = jnp.zeros((N, N), f32)
    for q in range(16):
        tile = state[q // 4, q % 4]
        row_edges[0, q : q + 1, :] = tile[0:1]
        row_edges[1, q : q + 1, :] = tile[N - 1 : N]
        cols = jnp.where(lane == q, tile[:, 0:1], cols)
        cols = jnp.where(lane == 16 + q, tile[:, N - 1 : N], cols)
    cols = cols.T
    col_edges[0] = cols[0:16]
    col_edges[1] = cols[16:32]


def explicit(tile_of, halo_of, rate, kin, cross, z, f_out):
    i0, j0 = iota((N, N), 0), iota((N, N), 1)
    tiles, laps = [], []
    for s in range(4):
        t = tile_of(s, z)
        up, down, left, right = halo_of(s, z)
        xm = jnp.where(i0 == 0, up, pltpu.roll(t, 1, 0))
        xp = jnp.where(i0 == N - 1, down, pltpu.roll(t, N - 1, 0))
        ym = jnp.where(j0 == 0, left, pltpu.roll(t, 1, 1))
        yp = jnp.where(j0 == N - 1, right, pltpu.roll(t, N - 1, 1))
        tiles.append(t)
        laps.append(xm + xp + ym + yp - 4.0 * t)
    for j in range(4):
        react = kin[0, j] * tiles[0]
        mix = cross[0, j] * laps[0]
        for i in range(1, 4):
            react = react + kin[i, j] * tiles[i]
            mix = mix + cross[i, j] * laps[i]
        f_out[j, :, z * N : (z + 1) * N] = (
            tiles[j] + 0.5 * rate[j, z] * react + 0.25 * mix
        )


def send_rows(f_out, hx, send, pay, nx):
    k = lax.axis_index("row")
    for s in range(4):
        ends = dot3(hx[s], f_out[s])
        for z in range(4):
            q = 4 * s + z
            pay[0, q : q + 1, :] = ends[0:1, z * N : (z + 1) * N]
            pay[1, q : q + 1, :] = ends[1:2, z * N : (z + 1) * N]
    a, b = pay[0], pay[1]
    for j in range(nx):
        send[j] = jnp.where(j > k, a, b)


def first_kernel(nx, state, rate, up, down, left, right, hx, kin, cross, f_out, send, cols, pay):
    zero = jnp.zeros((N - 32, N), f32)
    cols[...] = jnp.concatenate([left[...], right[...], zero], axis=0).T

    def halo_of(s, z):
        q = 4 * s + z
        return (
            up[q : q + 1, :],
            down[q : q + 1, :],
            cols[:, q : q + 1],
            cols[:, 16 + q : 17 + q],
        )

    for z in range(4):
        explicit(lambda s, z: state[s, z], halo_of, rate, kin, cross, z, f_out)
    send_rows(f_out, hx, send, pay, nx)


def rows_kernel(nx, ny, f_in, recv, wx, gx, lx, hy, g_out, send, pay):
    l = lax.axis_index("col")
    incoming = dot3(wx[...], recv[...].reshape(nx * 16, N))
    pay[...] = jnp.zeros_like(pay)
    for s in range(4):
        g = dot3(gx[s], f_in[s])
        lam, mu = lx[s, :, 0:1], lx[s, :, 1:2]
        parts, tails = [], []
        for z in range(4):
            q = 4 * s + z
            part = (
                g[:, z * N : (z + 1) * N]
                + lam * incoming[q : q + 1]
                + mu * incoming[16 + q : 17 + q]
            )
            g_out[s, z] = part
            parts.append(part[0:N])
            tails.append(part[N:EXT])
        ends = dot3(hy[s], jnp.concatenate(parts + tails, axis=0), nt=True)
        for p in range(2):
            for z in range(4):
                q = 4 * s + z
                pay[p, q : q + 1, :] = ends[p : p + 1, z * N : (z + 1) * N]
            pay[p, 16 + s : 17 + s, 0:32] = ends[p : p + 1, 4 * N : 4 * N + 32]
    a, b = pay[0], pay[1]
    for m in range(ny):
        send[m] = jnp.where(m > l, a, b)


def cols_part(ny, g_in, recv, wy, gy, ry, s, turned, wide):
    width = 2 * N if wide else N
    g = g_in[s].reshape(4 * EXT, N)
    out = dot3(g, gy[s, :, 0:width])
    lam, mu = ry[s, 0:1, 0:width], ry[s, 1:2, 0:width]
    result = []
    for z in range(4):
        q = 4 * s + z

        def column(p):
            main = turned[:, 16 * p + q : 16 * p + q + 1]
            tail = turned[8 * z : 8 * z + 8, 32 + 4 * p + s : 33 + 4 * p + s]
            return jnp.concatenate([main, tail], axis=0)

        result.append(
            out[z * EXT : (z + 1) * EXT] + column(0) * lam + column(1) * mu
        )
    return result


def turned_of(ny, recv, wy, turned):
    incoming = dot3(wy[...], recv[...].reshape(ny * 24, N))
    turned[...] = jnp.concatenate([incoming, jnp.zeros((N - 40, N), f32)], axis=0).T


def next_kernel(nx, ny, g_in, recv, wy, gy, ry, rate, hx, kin, cross, f_out, send, st, turned, pay):
    turned_of(ny, recv, wy, turned)
    for s in range(4):
        parts = cols_part(ny, g_in, recv, wy, gy, ry, s, turned, True)
        for z in range(4):
            st[s, z] = parts[z]

    def halo_of(s, z):
        return (
            st[s, z, N : N + 1, 0:N],
            st[s, z, N + 1 : N + 2, 0:N],
            st[s, z, 0:N, N : N + 1],
            st[s, z, 0:N, N + 1 : N + 2],
        )

    for z in range(4):
        explicit(lambda s, z: st[s, z, 0:N, 0:N], halo_of, rate, kin, cross, z, f_out)
    send_rows(f_out, hx, send, pay, nx)


def last_kernel(ny, g_in, recv, wy, gy, ry, out, turned):
    turned_of(ny, recv, wy, turned)
    for s in range(4):
        parts = cols_part(ny, g_in, recv, wy, gy, ry, s, turned, False)
        for z in range(4):
            out[s, z] = parts[z][0:N]


def call(body, outs, scratch, smem=0, cost=3_000_000):
    shapes = [jax.ShapeDtypeStruct(shape, f32) for shape in outs]

    def run(*args):
        count = len(args) - smem
        return pl.pallas_call(
            body,
            out_shape=shapes,
            in_specs=[pl.BlockSpec(memory_space=pltpu.VMEM)] * count
            + [pl.BlockSpec(memory_space=pltpu.SMEM)] * smem,
            out_specs=[pl.BlockSpec(memory_space=pltpu.VMEM)] * len(shapes),
            scratch_shapes=[pltpu.VMEM(shape, f32) for shape in scratch],
            compiler_params=pltpu.CompilerParams(vmem_limit_bytes=VMEM),
            cost_estimate=pl.CostEstimate(
                flops=cost * 1000, bytes_accessed=cost, transcendentals=0
            ),
        )(*args)

    return run


def on_device(adjoint, rate_scale, kinetics, cross_matrix, x_diffusion, y_diffusion):
    nx, ny = lax.axis_size("row"), lax.axis_size("col")
    row_edges, col_edges = call(edges_kernel, [(2, 16, N), (2, 16, N)], [])(adjoint)
    up = lax.ppermute(row_edges[1], "row", [(i, i + 1) for i in range(nx - 1)])
    down = lax.ppermute(row_edges[0], "row", [(i + 1, i) for i in range(nx - 1)])
    left = lax.ppermute(col_edges[1], "col", [(i, i + 1) for i in range(ny - 1)])
    right = lax.ppermute(col_edges[0], "col", [(i + 1, i) for i in range(ny - 1)])
    gx, lx, hx, gy, ry, hy, wx, wy = call(
        functools.partial(tables_kernel, nx, ny),
        [
            (4, EXT, N), (4, EXT, N), (4, 8, N), (4, N, 2 * N), (4, 8, 2 * N), (4, 8, N),
            (32, nx * 16), (40, ny * 24),
        ],
        [(N, N)] * 8,
    )(x_diffusion, y_diffusion)
    f_shape, g_shape = (4, N, 4 * N), (4, 4, EXT, N)
    send_x, send_y = (nx, 16, N), (ny, 24, N)
    f, send = call(
        functools.partial(first_kernel, nx), [f_shape, send_x], [(N, N), (2, 16, N)], 2
    )(adjoint, rate_scale, up, down, left, right, hx, kinetics, cross_matrix)
    for step in range(STEPS):
        recv = lax.all_to_all(send, "row", 0, 0, tiled=True)
        g, send = call(
            functools.partial(rows_kernel, nx, ny), [g_shape, send_y], [(2, 24, N)]
        )(f, recv, wx, gx, lx, hy)
        recv = lax.all_to_all(send, "col", 0, 0, tiled=True)
        if step + 1 < STEPS:
            f, send = call(
                functools.partial(next_kernel, nx, ny),
                [f_shape, send_x],
                [(4, 4, EXT, 2 * N), (N, N), (2, 16, N)],
                2,
            )(g, recv, wy, gy, ry, rate_scale, hx, kinetics, cross_matrix)
        else:
            (out,) = call(functools.partial(last_kernel, ny), [(4, 4, N, N)], [(N, N)])(
                g, recv, wy, gy, ry
            )
    return out


def solution(mesh):
    return jax.shard_map(
        on_device,
        mesh=mesh,
        in_specs=(P(None, None, "row", "col"), P(None, None, "row", "col"), P(), P(), P(), P()),
        out_specs=P(None, None, "row", "col"),
        check_vma=False,
    )
```

```python
import functools

import jax
import jax.numpy as jnp
from jax import lax
from jax.experimental import pallas as pl
from jax.experimental.pallas import tpu as pltpu
from jax.sharding import PartitionSpec as P

M = 1000.0
N = 128
EXT = N + 8
f32 = jnp.float32
bf16 = jnp.bfloat16
VMEM = 20 * 1024 * 1024


def iota(shape, dim):
    return lax.broadcasted_iota(jnp.int32, shape, dim)


def split(a):
    hi = a.astype(bf16)
    return hi, (a - hi.astype(f32)).astype(bf16)


def dot3(a, b, nt=False):
    dims = (((1,), (1 if nt else 0,)), ((), ()))
    ah, al = split(a)
    bh, bl = split(b)

    def dot(p, q):
        return lax.dot_general(p, q, dims, preferred_element_type=f32)

    return dot(ah, bh) + (dot(ah, bl) + dot(al, bh))


def tables_kernel(
    nx, ny, xd, yd, gx, lx, hx, gy, ry, hy, wx, wx_cols, wy, wy_last,
    rows_x, rows_y, ex, ey, p0, p1, q0, q1,
):
    k = lax.axis_index("row")
    l = lax.axis_index("col")
    scale = 1.0 / M
    rows_x[...] = jnp.full((N, N), scale, f32)
    rows_y[...] = jnp.full((N, N), scale, f32)
    for j in range(nx):
        rows_x[4 * j : 4 * j + 4, :] = scale / xd[:, j * N : (j + 1) * N]
    for j in range(ny):
        rows_y[4 * j : 4 * j + 4, :] = scale / yd[:, j * N : (j + 1) * N]

    def block(ref, index):
        return scale / ref[:, pl.ds(pl.multiple_of(index * N, N), N)]

    rows_y[32:36, :] = block(xd, k)
    rows_y[36:40, :] = block(yd, l)
    rows_y[40:44, :] = block(xd, jnp.maximum(k - 1, 0)) * (k > 0).astype(f32)
    rows_y[44:48, :] = block(yd, jnp.maximum(l - 1, 0)) * (l > 0).astype(f32)
    rows_y[48:52, :] = block(xd, jnp.minimum(k + 1, nx - 1)) * (k < nx - 1).astype(f32)
    rows_y[52:56, :] = block(yd, jnp.minimum(l + 1, ny - 1)) * (l < ny - 1).astype(f32)
    ex[...] = rows_x[...].T
    ey[...] = rows_y[...].T

    first2 = (iota((2, N), 0) == 0).astype(f32)
    one, zero = jnp.ones((1, N), f32), jnp.zeros((1, N), f32)

    def body(i, carry):
        vx, dx, va, da, vb, db, ux, cx, ua, ca, ub, cb = carry
        at = pl.multiple_of(i * 8, 8)
        back = pl.multiple_of(N - 8 - i * 8, 8)
        ex_f, ey_f = ex[pl.ds(at, 8), :], ey[pl.ds(at, 8), :]
        ex_b, ey_b = ex[pl.ds(back, 8), :], ey[pl.ds(back, 8), :]
        for r in range(8):
            t = at + r
            p0[pl.ds(t, 1), :] = va
            p1[pl.ds(t, 1), :] = vb
            e, ee = ex_f[r : r + 1], ey_f[r : r + 1]
            dx = dx + e * vx
            vx = vx + dx
            da = da + ee * va
            va = va + da
            db = db + ee * vb
            vb = vb + db
            r2 = 7 - r
            t = back + r2
            q0[pl.ds(t, 1), :] = ua
            q1[pl.ds(t, 1), :] = ub
            e, ee = ex_b[r2 : r2 + 1], ey_b[r2 : r2 + 1]
            cx = cx + e * ux
            ux = ux + cx
            ca = ca + ee * ua
            ua = ua + ca
            cb = cb + ee * ub
            ub = ub + cb
        return vx, dx, va, da, vb, db, ux, cx, ua, ca, ub, cb

    init = (first2, 1.0 - first2, one, zero, zero, one)
    vx, dx, va, da, vb, db, ux, cx, ua, ca, ub, cb = lax.fori_loop(
        0, N // 8, body, init + init
    )

    row = iota((8, N), 0)
    lane = iota((8, N), 1)
    blk = lane // 4
    forward = row < 2
    is_x = row % 2 == 0
    count = jnp.where(is_x, nx, ny)
    own = jnp.where(is_x, k, l)
    place = jnp.where(forward, blk, count - 1 - blk)
    own = jnp.where(forward, own, count - 1 - own)

    def pack(a, b, c, d):
        return jnp.where(
            row == 0, a, jnp.where(row == 1, b, jnp.where(row == 2, c, d))
        )

    def shifted(a, by):
        return jnp.where(
            forward, pltpu.roll(a, 4 * by, 1), pltpu.roll(a, N - 4 * by, 1)
        )

    def outside(by):
        return place < by

    a0 = pack(vx[0:1], va, ux[0:1], ua)
    b0 = pack(vx[1:2], vb, ux[1:2], ub)
    c0 = pack(dx[0:1], da, cx[0:1], ca)
    d0 = pack(dx[1:2], db, cx[1:2], cb)
    a, b, c, d = a0, b0, c0, d0
    by = 1
    while by < max(nx, ny):
        skip = outside(by)
        sa = jnp.where(skip, 1.0, shifted(a, by))
        sb = jnp.where(skip, 0.0, shifted(b, by))
        sc = jnp.where(skip, 0.0, shifted(c, by))
        sd = jnp.where(skip, 1.0, shifted(d, by))
        a, b, c, d = a * sa + b * sc, a * sb + b * sd, c * sa + d * sc, c * sb + d * sd
        norm = 1.0 / (a + b)
        a, b, c, d = a * norm, b * norm, c * norm, d * norm
        by *= 2
    skip = outside(1)
    slope = jnp.where(skip, 1.0, shifted((c + d) / (a + b), 1))

    decay = (1.0 - slope) / ((a0 + b0 * slope) - (c0 + d0 * slope))
    between = (place < own) & (place >= 0)
    prod = jnp.where(between, decay, 1.0)

    def against(a, by):
        return jnp.where(
            forward, pltpu.roll(a, N - 4 * by, 1), pltpu.roll(a, 4 * by, 1)
        )

    def past(by):
        return place + by >= count

    by = 1
    while by < max(nx, ny):
        prod = prod * jnp.where(past(by), 1.0, against(prod, by))
        by *= 2
    weight = jnp.where(between, jnp.where(past(1), 1.0, against(prod, 1)), 0.0)

    def expand(width, per_block, species_of):
        src = iota((N, width), 0)
        col = iota((N, width), 1)
        hit = (src // 4 == col // per_block) & (src % 4 == species_of(col % per_block))
        return lax.dot_general(
            weight,
            jnp.where(hit, 1.0, 0.0),
            (((1,), (0,)), ((), ())),
            precision=lax.Precision.HIGHEST,
            preferred_element_type=f32,
        )

    width = nx * 16
    spread = expand(width, 16, lambda r: r // 4)
    rr, cc = iota((32, width), 0), iota((32, width), 1)
    wx[...] = jnp.where(
        rr % 16 == cc % 16, jnp.where(rr < 16, spread[0:1], spread[2:3]), 0.0
    )
    width = nx * 8
    spread = expand(width, 8, lambda r: r)
    rr, cc = iota((16, width), 0), iota((16, width), 1)
    wx_cols[...] = jnp.where(
        rr % 8 == cc % 8, jnp.where(rr < 8, spread[0:1], spread[2:3]), 0.0
    )
    width = ny * 24
    spread = expand(width, 24, lambda r: jnp.where(r < 16, r // 4, r - 16))
    rr, cc = iota((48, width), 0), iota((48, width), 1)
    hit = jnp.where(rr < 32, rr % 16, 16 + rr % 8) == cc % 24
    left = (rr < 16) | ((rr >= 32) & (rr < 40))
    wy[...] = jnp.where(hit, jnp.where(left, spread[1:2], spread[3:4]), 0.0)

    width = ny * 16
    spread = expand(width, 16, lambda r: r // 4)
    rr, cc = iota((32, width), 0), iota((32, width), 1)
    wy_last[...] = jnp.where(
        rr % 16 == cc % 16, jnp.where(rr < 16, spread[1:2], spread[3:4]), 0.0
    )

    lane1 = iota((1, N), 1)
    to_x = lax.rem(32 - 4 * k + N, N)
    to_y = lax.rem(36 - 4 * l + N, N)
    sx = pltpu.roll(slope, to_x, 1)
    sy = pltpu.roll(slope, to_y, 1)
    valid = (lane1 >= 32) & (lane1 < 40)
    sf = jnp.where(valid, jnp.where(lane1 < 36, sx[0:1], sy[1:2]), 1.0)
    sb = jnp.where(valid, jnp.where(lane1 < 36, sx[2:3], sy[3:4]), 1.0)
    phi = p0[...] + p1[...] * sf
    psi = q0[...] + q1[...] * sb
    phi_before, phi_after = 1.0 - sf, va + vb * sf
    psi_after, psi_before = 1.0 - sb, ua + ub * sb
    wron = sf * psi_before + (ca + cb * sb) * phi_before
    inv_w = 1.0 / wron
    psi = psi * inv_w
    psi_after, psi_before = psi_after * inv_w, psi_before * inv_w
    phi_t, psi_t = phi.T, psi.T
    eps = ey[...]
    eps_t = rows_y[...]
    i0, j0 = iota((N, N), 0), iota((N, N), 1)
    low = i0 >= j0
    r8 = iota((8, N), 0)
    c8 = iota((8, N), 1)
    for s in range(4):
        n = 32 + s
        e_b, e_a = eps_t[40 + s : 41 + s, N - 1 : N], eps_t[48 + s : 49 + s, 0:1]
        at = slice(n, n + 1)
        pr, qr = phi_t[at], psi_t[at]
        pc, qc, ec = phi[:, at], psi[:, at], eps[:, at]
        pb, pa, qb, qa = phi_before[:, at], phi_after[:, at], psi_before[:, at], psi_after[:, at]
        gx[s, 0:N, :] = jnp.where(low, (ec * qc) * pr, (ec * pc) * qr)
        gx[s, N:EXT, :] = jnp.where(
            r8 == 0, (e_b * pb) * qr, jnp.where(r8 == 1, (e_a * qa) * pr, 0.0)
        )
        lx[s, 0:N, :] = jnp.where(
            j0 == 0, ec * qc * pb, jnp.where(j0 == 1, ec * pc * qa, 0.0)
        )
        before = jnp.where(c8 == 0, e_b * pb * qb, e_b * pb * qa)
        after = jnp.where(c8 == 0, e_a * pb * qa, e_a * pa * qa)
        lx[s, N:EXT, :] = jnp.where(
            (r8 < 2) & (c8 < 2), jnp.where(r8 == 0, before, after), 0.0
        )
        inv_p, inv_q = 1.0 / pr[:, N - 1 : N], 1.0 / qr[:, 0:1]
        beside = jnp.where(
            c8 == 0,
            pb * inv_p,
            jnp.where(c8 == 1, pa * inv_p, jnp.where(c8 == 2, qb * inv_q, qa * inv_q)),
        )
        hx[s] = jnp.where(
            r8 == 0,
            pr * inv_p,
            jnp.where(r8 == 1, qr * inv_q, jnp.where(r8 == 2, beside, 0.0)),
        )

        n = 36 + s
        e_b, e_a = eps_t[44 + s : 45 + s, N - 1 : N], eps_t[52 + s : 53 + s, 0:1]
        at = slice(n, n + 1)
        pr, qr, er = phi_t[at], psi_t[at], eps_t[at]
        pc, qc = phi[:, at], psi[:, at]
        pb, pa, qb, qa = phi_before[:, at], phi_after[:, at], psi_before[:, at], psi_after[:, at]
        gy[s, :, 0:N] = jnp.where(low, qc * (pr * er), pc * (qr * er))
        gy[s, :, N:] = jnp.where(
            j0 == 0, qc * (pb * e_b), jnp.where(j0 == 1, pc * (qa * e_a), 0.0)
        )
        ry[s, :, 0:N] = jnp.where(
            r8 == 0, pb * qr * er, jnp.where(r8 == 1, qa * pr * er, 0.0)
        )
        before = jnp.where(r8 == 0, e_b * pb * qb, e_b * pb * qa)
        after = jnp.where(r8 == 0, e_a * pb * qa, e_a * pa * qa)
        ry[s, :, N:] = jnp.where(
            (r8 < 2) & (c8 < 2), jnp.where(c8 == 0, before, after), 0.0
        )
        inv_p, inv_q = 1.0 / pr[:, N - 1 : N], 1.0 / qr[:, 0:1]
        hy[s, :, 0:N] = jnp.where(
            r8 < 4, jnp.where(r8 % 2 == 0, pr * inv_p, qr * inv_q), 0.0
        )
        before = jnp.where(
            (r8 == 0) | (r8 == 2),
            pb * inv_p,
            jnp.where(r8 == 3, qb * inv_q, jnp.where(r8 == 4, 1.0, 0.0)),
        )
        after = jnp.where(
            (r8 == 1) | (r8 == 3),
            qa * inv_q,
            jnp.where(r8 == 2, pa * inv_p, jnp.where(r8 == 5, 1.0, 0.0)),
        )
        hy[s, :, N:] = jnp.where(c8 == 0, before, jnp.where(c8 == 1, after, 0.0))


def explicit(tile_of, halo_of, rate, kin, cross, z, f_out):
    i0, j0 = iota((N, N), 0), iota((N, N), 1)
    tiles, laps = [], []
    for s in range(4):
        t = tile_of(s, z)
        up, down, left, right = halo_of(s, z)
        xm = jnp.where(i0 == 0, up, pltpu.roll(t, 1, 0))
        xp = jnp.where(i0 == N - 1, down, pltpu.roll(t, N - 1, 0))
        ym = jnp.where(j0 == 0, left, pltpu.roll(t, 1, 1))
        yp = jnp.where(j0 == N - 1, right, pltpu.roll(t, N - 1, 1))
        tiles.append(t)
        laps.append(xm + xp + ym + yp - 4.0 * t)
    for j in range(4):
        react = kin[0, j] * tiles[0]
        mix = cross[0, j] * laps[0]
        for i in range(1, 4):
            react = react + kin[i, j] * tiles[i]
            mix = mix + cross[i, j] * laps[i]
        f_out[j, :, z * N : (z + 1) * N] = (
            tiles[j] + 0.5 * rate[j, z] * react + 0.25 * mix
        )


def line_sums(f_out, hx, s):
    ends = dot3(hx[s], f_out[s])
    return ends[0:1], ends[1:2]


def by_plane(ref, p, s, values):
    for z in range(4):
        q = 4 * s + z
        ref[p, q : q + 1, :] = values[:, z * N : (z + 1) * N]


def send_rows(f_out, hx, send, pay, nx):
    k = lax.axis_index("row")
    for s in range(4):
        a, b = line_sums(f_out, hx, s)
        by_plane(pay, 0, s, a)
        by_plane(pay, 1, s, b)
    for j in range(nx):
        send[j] = pay[(j < k).astype(jnp.int32)]


def message(j, own):
    return jnp.where(j > own, 0, 1) + jnp.where((j == own + 1) | (j == own - 1), 0, 2)


def first_kernel(nx, ny, state, rate, hx, kin, cross, f_out, send, cells, cols, pay):
    k, l = lax.axis_index("row"), lax.axis_index("col")
    none = (0.0, 0.0, 0.0, 0.0)
    for z in range(4):
        explicit(lambda s, z: state[s, z], lambda s, z: none, rate, kin, cross, z, f_out)

    lane = iota((N, N), 1)
    side = []
    for s in range(4):
        acc = jnp.zeros((N, N), f32)
        for z in range(4):
            tile = state[s, z]
            acc = jnp.where(lane == 8 * z, tile[:, 0:1], acc)
            acc = jnp.where(lane == 8 * z + 1, tile[:, N - 1 : N], acc)
        side.append(acc)
    has = jnp.where(lane % 8 == 0, (l > 0).astype(f32), (l < ny - 1).astype(f32))
    before_x = 0.25 * (k > 0).astype(f32)
    after_x = 0.25 * (k < nx - 1).astype(f32)
    pay[...] = jnp.zeros_like(pay)
    for j in range(4):
        mix = cross[0, j] * side[0]
        for i in range(1, 4):
            mix = mix + cross[i, j] * side[i]
        mix = 0.25 * has * mix
        cols[j] = mix
        for z in range(4):
            q = 4 * j + z
            low = cross[0, j] * state[0, z, 0:1, :]
            high = cross[0, j] * state[0, z, N - 1 : N, :]
            for i in range(1, 4):
                low = low + cross[i, j] * state[i, z, 0:1, :]
                high = high + cross[i, j] * state[i, z, N - 1 : N, :]
            cells[0, q : q + 1, :] = before_x * low
            cells[1, q : q + 1, :] = after_x * high
        a, b = line_sums(f_out, hx, j)
        before = jnp.concatenate([cells[0, 4 * j + z : 4 * j + z + 1, :] for z in range(4)], axis=1)
        after = jnp.concatenate([cells[1, 4 * j + z : 4 * j + z + 1, :] for z in range(4)], axis=1)
        p_b, p_a = hx[j, 2:3, 0:1], hx[j, 2:3, 1:2]
        q_b, q_a = hx[j, 2:3, 2:3], hx[j, 2:3, 3:4]
        a = a + p_b * before
        b = b + q_a * after
        by_plane(pay, 0, j, a)
        by_plane(pay, 1, j, b)
        by_plane(pay, 2, j, a + p_a * after)
        by_plane(pay, 3, j, b + q_b * before)
        ends = dot3(hx[j], mix)
        for p in range(4):
            pay[p, 32 + j : 33 + j, :] = ends[p % 2 : p % 2 + 1]
    for p in range(4):
        pay[p, 16:32, :] = cells[1 - p % 2]
    for j in range(nx):
        send[j] = pay[message(j, k)]


def first_rows_kernel(
    nx, ny, f_in, cells, cols, recv, wx, wx_cols, gx, lx, hy, g_out, send, beside, pay
):
    k, l = lax.axis_index("row"), lax.axis_index("col")
    incoming = dot3(wx[...], recv[:, 0:16, :].reshape(nx * 16, N))
    in_cols = dot3(wx_cols[...], recv[:, 32:40, :].reshape(nx * 8, N))
    from_before = incoming[0:16] + cells[0]
    from_after = incoming[16:32] + cells[1]
    at_first = recv[jnp.maximum(k - 1, 0), 16:32, :] * (k > 0).astype(f32)
    at_last = recv[jnp.minimum(k + 1, nx - 1), 16:32, :] * (k < nx - 1).astype(f32)
    pay[...] = jnp.zeros_like(pay)
    for s in range(4):
        g = dot3(gx[s], f_in[s])
        lam, mu = lx[s, :, 0:1], lx[s, :, 1:2]
        col = (
            dot3(gx[s], cols[s])
            + lam * in_cols[s : s + 1]
            + mu * in_cols[8 + s : 9 + s]
        )
        first, last = gx[s, :, 0:1], gx[s, :, N - 1 : N]
        parts, tails = [], []
        for z in range(4):
            q = slice(4 * s + z, 4 * s + z + 1)
            part = (
                g[:, z * N : (z + 1) * N]
                + lam * from_before[q]
                + mu * from_after[q]
                + first * at_first[q]
                + last * at_last[q]
            )
            g_out[s, z] = part
            part = jnp.concatenate(
                [part, col if z == 0 else pltpu.roll(col, N - 8 * z, 1)], axis=1
            )
            parts.append(part[0:N])
            tails.append(part[N:EXT])
        ends = dot3(hy[s], jnp.concatenate(parts + tails, axis=0), nt=True)
        for p in range(6):
            by_plane(pay, p, s, ends[p : p + 1, 0 : 4 * N])
            pay[p, 16 + s : 17 + s, 0:32] = ends[p : p + 1, 4 * N : 4 * N + 32]
    beside[0] = pay[4]
    beside[1] = pay[5]
    for m in range(ny):
        send[m, 0:24] = pay[message(m, l)]
        send[m, 24:48] = pay[4 + jnp.where(m > l, 1, 0)]


def rows_kernel(nx, ny, f_in, recv, wx, gx, lx, hy, g_out, send, pay):
    l = lax.axis_index("col")
    incoming = dot3(wx[...], recv[...].reshape(nx * 16, N))
    pay[...] = jnp.zeros_like(pay)
    for s in range(4):
        g = dot3(gx[s], f_in[s])
        lam, mu = lx[s, :, 0:1], lx[s, :, 1:2]
        parts = []
        for z in range(4):
            q = 4 * s + z
            part = (
                g[0:N, z * N : (z + 1) * N]
                + lam[0:N] * incoming[q : q + 1]
                + mu[0:N] * incoming[16 + q : 17 + q]
            )
            g_out[s, z] = part
            parts.append(part)
        ends = dot3(hy[s, :, 0:N], jnp.concatenate(parts, axis=0), nt=True)
        for p in range(2):
            by_plane(pay, p, s, ends[p : p + 1])
    for m in range(ny):
        send[m] = pay[(m < l).astype(jnp.int32)]


def outer_sum(out, turned, pairs, q, s):
    for main, tail, row in pairs:
        col = turned[:, main + q : main + q + 1]
        if tail is not None:
            at = 8 * (q % 4)
            col = jnp.concatenate(
                [col, turned[at : at + 8, tail + s : tail + s + 1]], axis=0
            )
        out = out + col * row
    return out


def next_kernel(
    nx, ny, g_in, recv, beside, wy, gy, ry, rate, hx, kin, cross, f_out, send, st, turned, pay
):
    l = lax.axis_index("col")
    incoming = dot3(wy[...], recv[:, 0:24, :].reshape(ny * 24, N))
    at_first = recv[jnp.maximum(l - 1, 0), 24:48, :] * (l > 0).astype(f32)
    at_last = recv[jnp.minimum(l + 1, ny - 1), 24:48, :] * (l < ny - 1).astype(f32)
    turned[...] = jnp.concatenate(
        [
            incoming[0:16] + beside[0, 0:16, :],
            incoming[16:32] + beside[1, 0:16, :],
            incoming[32:40] + beside[0, 16:24, :],
            incoming[40:48] + beside[1, 16:24, :],
            at_first,
            at_last,
            jnp.zeros((N - 96, N), f32),
        ],
        axis=0,
    ).T
    for s in range(4):
        out = dot3(g_in[s].reshape(4 * EXT, N), gy[s])
        pairs = [
            (0, 32, ry[s, 0:1]),
            (16, 40, ry[s, 1:2]),
            (48, 64, gy[s, 0:1]),
            (72, 88, gy[s, N - 1 : N]),
        ]
        for z in range(4):
            st[s, z] = outer_sum(out[z * EXT : (z + 1) * EXT], turned, pairs, 4 * s + z, s)

    def halo_of(s, z):
        return (
            st[s, z, N : N + 1, 0:N],
            st[s, z, N + 1 : N + 2, 0:N],
            st[s, z, 0:N, N : N + 1],
            st[s, z, 0:N, N + 1 : N + 2],
        )

    for z in range(4):
        explicit(lambda s, z: st[s, z, 0:N, 0:N], halo_of, rate, kin, cross, z, f_out)
    send_rows(f_out, hx, send, pay, nx)


def last_kernel(ny, g_in, recv, wy, gy, ry, out, turned):
    incoming = dot3(wy[...], recv[...].reshape(ny * 16, N))
    turned[...] = jnp.concatenate([incoming, jnp.zeros((N - 32, N), f32)], axis=0).T
    for s in range(4):
        res = dot3(g_in[s].reshape(4 * N, N), gy[s, :, 0:N])
        pairs = [(0, None, ry[s, 0:1, 0:N]), (16, None, ry[s, 1:2, 0:N])]
        for z in range(4):
            out[s, z] = outer_sum(res[z * N : (z + 1) * N], turned, pairs, 4 * s + z, s)


def call(body, outs, scratch, smem=0, cost=3_000_000):
    shapes = [jax.ShapeDtypeStruct(shape, f32) for shape in outs]

    def run(*args):
        count = len(args) - smem
        return pl.pallas_call(
            body,
            out_shape=shapes,
            in_specs=[pl.BlockSpec(memory_space=pltpu.VMEM)] * count
            + [pl.BlockSpec(memory_space=pltpu.SMEM)] * smem,
            out_specs=[pl.BlockSpec(memory_space=pltpu.VMEM)] * len(shapes),
            scratch_shapes=[pltpu.VMEM(shape, f32) for shape in scratch],
            compiler_params=pltpu.CompilerParams(vmem_limit_bytes=VMEM),
            cost_estimate=pl.CostEstimate(
                flops=cost * 1000, bytes_accessed=cost, transcendentals=0
            ),
        )(*args)

    return run


def on_device(adjoint, rate_scale, kinetics, cross_matrix, x_diffusion, y_diffusion):
    nx, ny = lax.axis_size("row"), lax.axis_size("col")
    part = functools.partial
    gx, lx, hx, gy, ry, hy, wx, wx_cols, wy, wy_last = call(
        part(tables_kernel, nx, ny),
        [
            (4, EXT, N), (4, EXT, N), (4, 8, N), (4, N, 2 * N), (4, 8, 2 * N), (4, 8, 2 * N),
            (32, nx * 16), (16, nx * 8), (48, ny * 24), (32, ny * 16),
        ],
        [(N, N)] * 8,
    )(x_diffusion, y_diffusion)
    f_shape = (4, N, 4 * N)
    f, send, cells, cols = call(
        part(first_kernel, nx, ny),
        [f_shape, (nx, 40, N), (2, 16, N), (4, N, N)],
        [(4, 40, N)],
        2,
    )(adjoint, rate_scale, hx, kinetics, cross_matrix)
    recv = lax.all_to_all(send, "row", 0, 0, tiled=True)
    g, send, beside = call(
        part(first_rows_kernel, nx, ny),
        [(4, 4, EXT, N), (ny, 48, N), (2, 24, N)],
        [(6, 24, N)],
    )(f, cells, cols, recv, wx, wx_cols, gx, lx, hy)
    recv = lax.all_to_all(send, "col", 0, 0, tiled=True)
    f, send = call(
        part(next_kernel, nx, ny),
        [f_shape, (nx, 16, N)],
        [(4, 4, EXT, 2 * N), (N, N), (2, 16, N)],
        2,
    )(g, recv, beside, wy, gy, ry, rate_scale, hx, kinetics, cross_matrix)
    recv = lax.all_to_all(send, "row", 0, 0, tiled=True)
    g, send = call(
        part(rows_kernel, nx, ny), [(4, 4, N, N), (ny, 16, N)], [(2, 16, N)]
    )(f, recv, wx, gx, lx, hy)
    recv = lax.all_to_all(send, "col", 0, 0, tiled=True)
    (out,) = call(part(last_kernel, ny), [(4, 4, N, N)], [(N, N)])(g, recv, wy_last, gy, ry)
    return out


def solution(mesh):
    return jax.shard_map(
        on_device,
        mesh=mesh,
        in_specs=(P(None, None, "row", "col"), P(None, None, "row", "col"), P(), P(), P(), P()),
        out_specs=P(None, None, "row", "col"),
        check_vma=False,
    )
```

```python
import functools

import jax
import jax.numpy as jnp
from jax import lax
from jax.experimental import pallas as pl
from jax.experimental.pallas import tpu as pltpu
from jax.sharding import PartitionSpec as P

M = 1000.0
STEPS = 2
N = 128
f32 = jnp.float32
bf16 = jnp.bfloat16
VMEM = 20 * 1024 * 1024


def iota(shape, dim):
    return lax.broadcasted_iota(jnp.int32, shape, dim)


def split(a):
    hi = a.astype(bf16)
    return hi, (a - hi.astype(f32)).astype(bf16)


def dot3(a, b, nt=False):
    dims = (((1,), (1 if nt else 0,)), ((), ()))
    ah, al = split(a)
    bh, bl = split(b)

    def dot(p, q):
        return lax.dot_general(p, q, dims, preferred_element_type=f32)

    return dot(ah, bh) + (dot(ah, bl) + dot(al, bh))


def tables_kernel(
    nx, ny, xd_in, yd_in, gx, lx, hx, gy, ry, hy, wx, wx_cols, wy,
    rows_x, rows_y, ex, ey, p0, p1, q0, q1, xd, yd, arrived,
):
    k = lax.axis_index("row")
    l = lax.axis_index("col")
    scale = 1.0 / M
    x_copy = pltpu.make_async_copy(xd_in, xd, arrived.at[0])
    y_copy = pltpu.make_async_copy(yd_in, yd, arrived.at[1])
    x_copy.start()
    y_copy.start()
    rows_x[...] = jnp.full((N, N), scale, f32)
    rows_y[...] = jnp.full((N, N), scale, f32)
    x_copy.wait()
    y_copy.wait()
    for j in range(nx):
        rows_x[4 * j : 4 * j + 4, :] = scale / xd[:, j * N : (j + 1) * N]
    for j in range(ny):
        rows_y[4 * j : 4 * j + 4, :] = scale / yd[:, j * N : (j + 1) * N]

    def block(ref, index):
        return scale / ref[:, pl.ds(pl.multiple_of(index * N, N), N)]

    rows_y[32:36, :] = block(xd, k)
    rows_y[36:40, :] = block(yd, l)
    ex[...] = rows_x[...].T
    ey[...] = rows_y[...].T

    first2 = (iota((2, N), 0) == 0).astype(f32)
    one, zero = jnp.ones((1, N), f32), jnp.zeros((1, N), f32)

    def body(i, carry):
        vx, dx, va, da, vb, db, ux, cx, ua, ca, ub, cb = carry
        at = pl.multiple_of(i * 8, 8)
        back = pl.multiple_of(N - 8 - i * 8, 8)
        ex_f, ey_f = ex[pl.ds(at, 8), :], ey[pl.ds(at, 8), :]
        ex_b, ey_b = ex[pl.ds(back, 8), :], ey[pl.ds(back, 8), :]
        for r in range(8):
            t = at + r
            p0[pl.ds(t, 1), :] = va
            p1[pl.ds(t, 1), :] = vb
            e, ee = ex_f[r : r + 1], ey_f[r : r + 1]
            dx = dx + e * vx
            vx = vx + dx
            da = da + ee * va
            va = va + da
            db = db + ee * vb
            vb = vb + db
            r2 = 7 - r
            t = back + r2
            q0[pl.ds(t, 1), :] = ua
            q1[pl.ds(t, 1), :] = ub
            e, ee = ex_b[r2 : r2 + 1], ey_b[r2 : r2 + 1]
            cx = cx + e * ux
            ux = ux + cx
            ca = ca + ee * ua
            ua = ua + ca
            cb = cb + ee * ub
            ub = ub + cb
        return vx, dx, va, da, vb, db, ux, cx, ua, ca, ub, cb

    init = (first2, 1.0 - first2, one, zero, zero, one)
    vx, dx, va, da, vb, db, ux, cx, ua, ca, ub, cb = lax.fori_loop(
        0, N // 8, body, init + init
    )

    row = iota((8, N), 0)
    lane = iota((8, N), 1)
    blk = lane // 4
    forward = row < 2
    is_x = row % 2 == 0
    count = jnp.where(is_x, nx, ny)
    own = jnp.where(is_x, k, l)
    place = jnp.where(forward, blk, count - 1 - blk)
    own = jnp.where(forward, own, count - 1 - own)

    def pack(a, b, c, d):
        return jnp.where(
            row == 0, a, jnp.where(row == 1, b, jnp.where(row == 2, c, d))
        )

    def shifted(a, by):
        return jnp.where(
            forward, pltpu.roll(a, 4 * by, 1), pltpu.roll(a, N - 4 * by, 1)
        )

    def outside(by):
        return place < by

    a0 = pack(vx[0:1], va, ux[0:1], ua)
    b0 = pack(vx[1:2], vb, ux[1:2], ub)
    c0 = pack(dx[0:1], da, cx[0:1], ca)
    d0 = pack(dx[1:2], db, cx[1:2], cb)
    a, b, c, d = a0, b0, c0, d0
    by = 1
    while by < max(nx, ny):
        skip = outside(by)
        sa = jnp.where(skip, 1.0, shifted(a, by))
        sb = jnp.where(skip, 0.0, shifted(b, by))
        sc = jnp.where(skip, 0.0, shifted(c, by))
        sd = jnp.where(skip, 1.0, shifted(d, by))
        a, b, c, d = a * sa + b * sc, a * sb + b * sd, c * sa + d * sc, c * sb + d * sd
        norm = 1.0 / (a + b)
        a, b, c, d = a * norm, b * norm, c * norm, d * norm
        by *= 2
    skip = outside(1)
    slope = jnp.where(skip, 1.0, shifted((c + d) / (a + b), 1))

    decay = (1.0 - slope) / ((a0 + b0 * slope) - (c0 + d0 * slope))
    between = (place < own) & (place >= 0)
    prod = jnp.where(between, decay, 1.0)

    def against(a, by):
        return jnp.where(
            forward, pltpu.roll(a, N - 4 * by, 1), pltpu.roll(a, 4 * by, 1)
        )

    def past(by):
        return place + by >= count

    by = 1
    while by < max(nx, ny):
        prod = prod * jnp.where(past(by), 1.0, against(prod, by))
        by *= 2
    weight = jnp.where(between, jnp.where(past(1), 1.0, against(prod, 1)), 0.0)

    def expand(width, per_block, species_of):
        src = iota((N, width), 0)
        col = iota((N, width), 1)
        hit = (src // 4 == col // per_block) & (src % 4 == species_of(col % per_block))
        return lax.dot_general(
            weight,
            jnp.where(hit, 1.0, 0.0),
            (((1,), (0,)), ((), ())),
            precision=lax.Precision.HIGHEST,
            preferred_element_type=f32,
        )

    width = nx * 16
    spread = expand(width, 16, lambda r: r // 4)
    rr, cc = iota((32, width), 0), iota((32, width), 1)
    wx[...] = jnp.where(
        rr % 16 == cc % 16, jnp.where(rr < 16, spread[0:1], spread[2:3]), 0.0
    )
    width = nx * 8
    spread = expand(width, 8, lambda r: r)
    rr, cc = iota((16, width), 0), iota((16, width), 1)
    wx_cols[...] = jnp.where(
        rr % 8 == cc % 8, jnp.where(rr < 8, spread[0:1], spread[2:3]), 0.0
    )
    width = ny * 16
    spread = expand(width, 16, lambda r: r // 4)
    rr, cc = iota((32, width), 0), iota((32, width), 1)
    wy[...] = jnp.where(
        rr % 16 == cc % 16, jnp.where(rr < 16, spread[1:2], spread[3:4]), 0.0
    )

    lane1 = iota((1, N), 1)
    to_x = lax.rem(32 - 4 * k + N, N)
    to_y = lax.rem(36 - 4 * l + N, N)
    sx = pltpu.roll(slope, to_x, 1)
    sy = pltpu.roll(slope, to_y, 1)
    valid = (lane1 >= 32) & (lane1 < 40)
    sf = jnp.where(valid, jnp.where(lane1 < 36, sx[0:1], sy[1:2]), 1.0)
    sb = jnp.where(valid, jnp.where(lane1 < 36, sx[2:3], sy[3:4]), 1.0)
    phi = p0[...] + p1[...] * sf
    psi = q0[...] + q1[...] * sb
    phi_before, phi_after = 1.0 - sf, va + vb * sf
    psi_after, psi_before = 1.0 - sb, ua + ub * sb
    wron = sf * psi_before + (ca + cb * sb) * phi_before
    inv_w = 1.0 / wron
    psi = psi * inv_w
    psi_after, psi_before = psi_after * inv_w, psi_before * inv_w
    phi_t, psi_t = phi.T, psi.T
    eps = ey[...]
    eps_t = rows_y[...]
    i0, j0 = iota((N, N), 0), iota((N, N), 1)
    low = i0 >= j0
    r8 = iota((8, N), 0)
    c8 = iota((8, N), 1)
    for s in range(4):
        at = slice(32 + s, 33 + s)
        pr, qr = phi_t[at], psi_t[at]
        pc, qc, ec = phi[:, at], psi[:, at], eps[:, at]
        pb, pa, qb, qa = phi_before[:, at], phi_after[:, at], psi_before[:, at], psi_after[:, at]
        eq, ep = ec * qc, ec * pc
        gx[s] = jnp.where(low, eq * pr, ep * qr)
        lx[s] = jnp.where(j0 == 0, eq * pb, jnp.where(j0 == 1, ep * qa, 0.0))
        inv_p, inv_q = 1.0 / pr[:, N - 1 : N], 1.0 / qr[:, 0:1]
        beside = jnp.where(
            c8 == 0,
            pb * inv_p,
            jnp.where(c8 == 1, pa * inv_p, jnp.where(c8 == 2, qb * inv_q, qa * inv_q)),
        )
        hx[s] = jnp.where(
            r8 == 0,
            pr * inv_p,
            jnp.where(r8 == 1, qr * inv_q, jnp.where(r8 == 2, beside, 0.0)),
        )

        at = slice(36 + s, 37 + s)
        pr, qr, er = phi_t[at], psi_t[at], eps_t[at]
        pc, qc = phi[:, at], psi[:, at]
        pb, pa, qb, qa = phi_before[:, at], phi_after[:, at], psi_before[:, at], psi_after[:, at]
        gy[s] = jnp.where(low, qc * (pr * er), pc * (qr * er))
        ry[s] = jnp.where(r8 == 0, pb * qr * er, jnp.where(r8 == 1, qa * pr * er, 0.0))
        inv_p, inv_q = 1.0 / pr[:, N - 1 : N], 1.0 / qr[:, 0:1]
        hy[s, :, 0:N] = jnp.where(
            r8 == 0, pr * inv_p, jnp.where(r8 == 1, qr * inv_q, 0.0)
        )
        before = jnp.where(
            r8 == 0, pb * inv_p, jnp.where(r8 == 1, qb * inv_q, jnp.where(r8 == 2, 1.0, 0.0))
        )
        after = jnp.where(
            r8 == 0, pa * inv_p, jnp.where(r8 == 1, qa * inv_q, jnp.where(r8 == 3, 1.0, 0.0))
        )
        hy[s, :, N:] = jnp.where(c8 == 0, before, jnp.where(c8 == 1, after, 0.0))


def by_plane(ref, p, s, values):
    for z in range(4):
        q = 4 * s + z
        ref[p, q : q + 1, :] = values[:, z * N : (z + 1) * N]


def explicit(nx, ny, state, rate, hx, kin, cross, f_out, send, cells, cols, pay):
    k, l = lax.axis_index("row"), lax.axis_index("col")
    i0, j0 = iota((N, N), 0), iota((N, N), 1)
    for z in range(4):
        tiles, laps = [], []
        for s in range(4):
            t = state[s, z]
            xm = jnp.where(i0 == 0, 0.0, pltpu.roll(t, 1, 0))
            xp = jnp.where(i0 == N - 1, 0.0, pltpu.roll(t, N - 1, 0))
            ym = jnp.where(j0 == 0, 0.0, pltpu.roll(t, 1, 1))
            yp = jnp.where(j0 == N - 1, 0.0, pltpu.roll(t, N - 1, 1))
            tiles.append(t)
            laps.append(xm + xp + ym + yp - 4.0 * t)
        for j in range(4):
            react = kin[0, j] * tiles[0]
            mix = cross[0, j] * laps[0]
            for i in range(1, 4):
                react = react + kin[i, j] * tiles[i]
                mix = mix + cross[i, j] * laps[i]
            f_out[j, :, z * N : (z + 1) * N] = (
                tiles[j] + 0.5 * rate[j, z] * react + 0.25 * mix
            )

    side = []
    for s in range(4):
        acc = jnp.zeros((N, N), f32)
        for z in range(4):
            tile = state[s, z]
            acc = jnp.where(j0 == 8 * z, tile[:, 0:1], acc)
            acc = jnp.where(j0 == 8 * z + 1, tile[:, N - 1 : N], acc)
        side.append(acc)
    has = jnp.where(j0 % 8 == 0, (l > 0).astype(f32), (l < ny - 1).astype(f32))
    has_x = 0.25 * (k > 0).astype(f32), 0.25 * (k < nx - 1).astype(f32)
    pay[...] = jnp.zeros_like(pay)
    for j in range(4):
        mix = cross[0, j] * side[0]
        for i in range(1, 4):
            mix = mix + cross[i, j] * side[i]
        mix = 0.25 * has * mix
        cols[j] = mix
        beside = []
        for p, row in enumerate((0, N - 1)):
            pieces = []
            for z in range(4):
                piece = cross[0, j] * state[0, z, row : row + 1, :]
                for i in range(1, 4):
                    piece = piece + cross[i, j] * state[i, z, row : row + 1, :]
                pieces.append(has_x[p] * piece)
            beside.append(jnp.concatenate(pieces, axis=1))
            by_plane(cells, p, j, beside[p])
        sums = dot3(hx[j], f_out[j])
        ends = dot3(hx[j], mix)
        for p in range(2):
            c = hx[j, 2:3, 2 * p : 2 * p + 1], hx[j, 2:3, 2 * p + 1 : 2 * p + 2]
            by_plane(pay, p, j, sums[p : p + 1] + c[0] * beside[0] + c[1] * beside[1])
            pay[p, 16 + j : 17 + j, :] = ends[p : p + 1]
    for j in range(nx):
        send[j] = pay[(j < k).astype(jnp.int32)]


def rows_kernel(
    nx, ny, f_in, cells, cols, recv, wx, wx_cols, gx, lx, hy, g_out, send, beside, pay
):
    l = lax.axis_index("col")
    incoming = dot3(wx[...], recv[:, 0:16, :].reshape(nx * 16, N))
    in_cols = dot3(wx_cols[...], recv[:, 16:24, :].reshape(nx * 8, N))
    from_before = incoming[0:16] + cells[0]
    from_after = incoming[16:32] + cells[1]
    for s in range(4):
        g = dot3(gx[s], f_in[s])
        lam, mu = lx[s, :, 0:1], lx[s, :, 1:2]
        col = (
            dot3(gx[s], cols[s])
            + lam * in_cols[s : s + 1]
            + mu * in_cols[8 + s : 9 + s]
        )
        parts = []
        for z in range(4):
            q = slice(4 * s + z, 4 * s + z + 1)
            part = (
                g[:, z * N : (z + 1) * N] + lam * from_before[q] + mu * from_after[q]
            )
            g_out[s, z] = part
            edge = col if z == 0 else pltpu.roll(col, N - 8 * z, 1)
            parts.append(jnp.concatenate([part, edge], axis=1))
        ends = dot3(hy[s], jnp.concatenate(parts, axis=0), nt=True)
        for p in range(2):
            by_plane(pay, p, s, ends[p : p + 1])
            by_plane(beside, p, s, ends[2 + p : 3 + p])
    for m in range(ny):
        send[m] = pay[(m < l).astype(jnp.int32)]


def finish_cols(ny, g_in, recv, beside, wy, gy, ry, out, turned):
    incoming = dot3(wy[...], recv[...].reshape(ny * 16, N))
    turned[...] = jnp.concatenate(
        [
            incoming[0:16] + beside[0],
            incoming[16:32] + beside[1],
            jnp.zeros((N - 32, N), f32),
        ],
        axis=0,
    ).T
    for s in range(4):
        res = dot3(g_in[s].reshape(4 * N, N), gy[s])
        lam, mu = ry[s, 0:1], ry[s, 1:2]
        for z in range(4):
            q = 4 * s + z
            out[s, z] = (
                res[z * N : (z + 1) * N]
                + turned[:, q : q + 1] * lam
                + turned[:, 16 + q : 17 + q] * mu
            )


def next_kernel(
    nx, ny, g_in, recv, beside, wy, gy, ry, rate, hx, kin, cross,
    f_out, send, cells, cols, state, turned, pay,
):
    finish_cols(ny, g_in, recv, beside, wy, gy, ry, state, turned)
    explicit(nx, ny, state, rate, hx, kin, cross, f_out, send, cells, cols, pay)


def call(body, outs, scratch, smem=0, place=pltpu.VMEM):
    shapes = [jax.ShapeDtypeStruct(shape, f32) for shape in outs]

    def run(*args):
        count = len(args) - smem
        return pl.pallas_call(
            body,
            out_shape=shapes,
            in_specs=[pl.BlockSpec(memory_space=place)] * count
            + [pl.BlockSpec(memory_space=pltpu.SMEM)] * smem,
            out_specs=[pl.BlockSpec(memory_space=pltpu.VMEM)] * len(shapes),
            scratch_shapes=[
                pltpu.VMEM(shape, f32) if isinstance(shape, tuple) else shape
                for shape in scratch
            ],
            compiler_params=pltpu.CompilerParams(vmem_limit_bytes=VMEM),
            cost_estimate=pl.CostEstimate(
                flops=3_000_000_000, bytes_accessed=3_000_000, transcendentals=0
            ),
        )(*args)

    return run


def on_device(adjoint, rate_scale, kinetics, cross_matrix, x_diffusion, y_diffusion):
    nx, ny = lax.axis_size("row"), lax.axis_size("col")
    part = functools.partial
    gx, lx, hx, gy, ry, hy, wx, wx_cols, wy = call(
        part(tables_kernel, nx, ny),
        [
            (4, N, N), (4, N, N), (4, 8, N), (4, N, N), (4, 8, N), (4, 8, 2 * N),
            (32, nx * 16), (16, nx * 8), (32, ny * 16),
        ],
        [(N, N)] * 8 + [x_diffusion.shape, y_diffusion.shape, pltpu.SemaphoreType.DMA((2,))],
        place=pl.ANY,
    )(x_diffusion, y_diffusion)
    tile = (4, 4, N, N)
    step_out = [(4, N, 4 * N), (nx, 24, N), (2, 16, N), (4, N, N)]
    f, send, cells, cols = call(part(explicit, nx, ny), step_out, [(2, 24, N)], 2)(
        adjoint, rate_scale, hx, kinetics, cross_matrix
    )
    for step in range(STEPS):
        recv = lax.all_to_all(send, "row", 0, 0, tiled=True)
        g, send, beside = call(
            part(rows_kernel, nx, ny), [tile, (ny, 16, N), (2, 16, N)], [(2, 16, N)]
        )(f, cells, cols, recv, wx, wx_cols, gx, lx, hy)
        recv = lax.all_to_all(send, "col", 0, 0, tiled=True)
        if step + 1 < STEPS:
            f, send, cells, cols = call(
                part(next_kernel, nx, ny), step_out, [tile, (N, N), (2, 24, N)], 2
            )(g, recv, beside, wy, gy, ry, rate_scale, hx, kinetics, cross_matrix)
    (out,) = call(part(finish_cols, ny), [tile], [(N, N)])(g, recv, beside, wy, gy, ry)
    return out


def solution(mesh):
    return jax.shard_map(
        on_device,
        mesh=mesh,
        in_specs=(P(None, None, "row", "col"), P(None, None, "row", "col"), P(), P(), P(), P()),
        out_specs=P(None, None, "row", "col"),
        check_vma=False,
    )
```

```python
import functools

import jax
import jax.numpy as jnp
from jax import lax
from jax.experimental import pallas as pl
from jax.experimental.pallas import tpu as pltpu
from jax.sharding import PartitionSpec as P

M = 1000.0
STEPS = 2
N = 128
f32 = jnp.float32
bf16 = jnp.bfloat16
VMEM = 20 * 1024 * 1024


def iota(shape, dim):
    return lax.broadcasted_iota(jnp.int32, shape, dim)


def split(a):
    hi = a.astype(bf16)
    return hi, (a - hi.astype(f32)).astype(bf16)


def dot3(a, b, nt=False):
    dims = (((1,), (1 if nt else 0,)), ((), ()))
    ah, al = split(a)
    bh, bl = split(b)

    def dot(p, q):
        return lax.dot_general(p, q, dims, preferred_element_type=f32)

    return dot(ah, bh) + (dot(ah, bl) + dot(al, bh))


def tables_kernel(
    nx, ny, xd_in, yd_in, gx, lx, rx, hx, gy, ry, hy, wx, wx_cols, wy,
    rows_x, rows_y, ex, ey, p0, p1, q0, q1, xd, yd, arrived,
):
    k = lax.axis_index("row")
    l = lax.axis_index("col")
    scale = 1.0 / M
    x_copy = pltpu.make_async_copy(xd_in, xd, arrived.at[0])
    y_copy = pltpu.make_async_copy(yd_in, yd, arrived.at[1])
    x_copy.start()
    y_copy.start()
    rows_x[...] = jnp.full((N, N), scale, f32)
    rows_y[...] = jnp.full((N, N), scale, f32)
    x_copy.wait()
    y_copy.wait()
    for j in range(nx):
        rows_x[4 * j : 4 * j + 4, :] = scale / xd[:, j * N : (j + 1) * N]
    for j in range(ny):
        rows_y[4 * j : 4 * j + 4, :] = scale / yd[:, j * N : (j + 1) * N]

    def block(ref, index):
        return scale / ref[:, pl.ds(pl.multiple_of(index * N, N), N)]

    rows_y[32:36, :] = block(xd, k)
    rows_y[36:40, :] = block(yd, l)
    ex[...] = rows_x[...].T
    ey[...] = rows_y[...].T

    first2 = (iota((2, N), 0) == 0).astype(f32)
    one, zero = jnp.ones((1, N), f32), jnp.zeros((1, N), f32)

    def body(i, carry):
        vx, dx, va, da, vb, db, ux, cx, ua, ca, ub, cb = carry
        at = pl.multiple_of(i * 8, 8)
        back = pl.multiple_of(N - 8 - i * 8, 8)
        ex_f, ey_f = ex[pl.ds(at, 8), :], ey[pl.ds(at, 8), :]
        ex_b, ey_b = ex[pl.ds(back, 8), :], ey[pl.ds(back, 8), :]
        for r in range(8):
            t = at + r
            p0[pl.ds(t, 1), :] = va
            p1[pl.ds(t, 1), :] = vb
            e, ee = ex_f[r : r + 1], ey_f[r : r + 1]
            dx = dx + e * vx
            vx = vx + dx
            da = da + ee * va
            va = va + da
            db = db + ee * vb
            vb = vb + db
            r2 = 7 - r
            t = back + r2
            q0[pl.ds(t, 1), :] = ua
            q1[pl.ds(t, 1), :] = ub
            e, ee = ex_b[r2 : r2 + 1], ey_b[r2 : r2 + 1]
            cx = cx + e * ux
            ux = ux + cx
            ca = ca + ee * ua
            ua = ua + ca
            cb = cb + ee * ub
            ub = ub + cb
        return vx, dx, va, da, vb, db, ux, cx, ua, ca, ub, cb

    init = (first2, 1.0 - first2, one, zero, zero, one)
    vx, dx, va, da, vb, db, ux, cx, ua, ca, ub, cb = lax.fori_loop(
        0, N // 8, body, init + init
    )

    row = iota((8, N), 0)
    lane = iota((8, N), 1)
    blk = lane // 4
    forward = row < 2
    is_x = row % 2 == 0
    count = jnp.where(is_x, nx, ny)
    own = jnp.where(is_x, k, l)
    place = jnp.where(forward, blk, count - 1 - blk)
    own = jnp.where(forward, own, count - 1 - own)

    def pack(a, b, c, d):
        return jnp.where(
            row == 0, a, jnp.where(row == 1, b, jnp.where(row == 2, c, d))
        )

    def shifted(a, by):
        return jnp.where(
            forward, pltpu.roll(a, 4 * by, 1), pltpu.roll(a, N - 4 * by, 1)
        )

    def outside(by):
        return place < by

    a0 = pack(vx[0:1], va, ux[0:1], ua)
    b0 = pack(vx[1:2], vb, ux[1:2], ub)
    c0 = pack(dx[0:1], da, cx[0:1], ca)
    d0 = pack(dx[1:2], db, cx[1:2], cb)
    a, b, c, d = a0, b0, c0, d0
    by = 1
    while by < max(nx, ny):
        skip = outside(by)
        sa = jnp.where(skip, 1.0, shifted(a, by))
        sb = jnp.where(skip, 0.0, shifted(b, by))
        sc = jnp.where(skip, 0.0, shifted(c, by))
        sd = jnp.where(skip, 1.0, shifted(d, by))
        a, b, c, d = a * sa + b * sc, a * sb + b * sd, c * sa + d * sc, c * sb + d * sd
        norm = 1.0 / (a + b)
        a, b, c, d = a * norm, b * norm, c * norm, d * norm
        by *= 2
    skip = outside(1)
    slope = jnp.where(skip, 1.0, shifted((c + d) / (a + b), 1))

    decay = (1.0 - slope) / ((a0 + b0 * slope) - (c0 + d0 * slope))
    between = (place < own) & (place >= 0)
    prod = jnp.where(between, decay, 1.0)

    def against(a, by):
        return jnp.where(
            forward, pltpu.roll(a, N - 4 * by, 1), pltpu.roll(a, 4 * by, 1)
        )

    def past(by):
        return place + by >= count

    by = 1
    while by < max(nx, ny):
        prod = prod * jnp.where(past(by), 1.0, against(prod, by))
        by *= 2
    weight = jnp.where(between, jnp.where(past(1), 1.0, against(prod, 1)), 0.0)

    def expand(width, per_block, species_of):
        src = iota((N, width), 0)
        col = iota((N, width), 1)
        hit = (src // 4 == col // per_block) & (src % 4 == species_of(col % per_block))
        return lax.dot_general(
            weight,
            jnp.where(hit, 1.0, 0.0),
            (((1,), (0,)), ((), ())),
            precision=lax.Precision.HIGHEST,
            preferred_element_type=f32,
        )

    width = nx * 16
    spread = expand(width, 16, lambda r: r // 4)
    rr, cc = iota((32, width), 0), iota((32, width), 1)
    wx[...] = jnp.where(
        rr % 16 == cc % 16, jnp.where(rr < 16, spread[0:1], spread[2:3]), 0.0
    )
    own_lanes = iota((nx, N), 1) // 4 == iota((nx, N), 0)
    by_species = jnp.where(iota((N, N), 0) % 4 == iota((N, N), 1), 1.0, 0.0)
    for p in range(2):
        wx_cols[p] = lax.dot_general(
            jnp.where(own_lanes, weight[2 * p : 2 * p + 1], 0.0),
            by_species,
            (((1,), (0,)), ((), ())),
            precision=lax.Precision.HIGHEST,
            preferred_element_type=f32,
        )
    width = ny * 16
    spread = expand(width, 16, lambda r: r // 4)
    rr, cc = iota((32, width), 0), iota((32, width), 1)
    wy[...] = jnp.where(
        rr % 16 == cc % 16, jnp.where(rr < 16, spread[1:2], spread[3:4]), 0.0
    )

    lane1 = iota((1, N), 1)
    to_x = lax.rem(32 - 4 * k + N, N)
    to_y = lax.rem(36 - 4 * l + N, N)
    sx = pltpu.roll(slope, to_x, 1)
    sy = pltpu.roll(slope, to_y, 1)
    valid = (lane1 >= 32) & (lane1 < 40)
    sf = jnp.where(valid, jnp.where(lane1 < 36, sx[0:1], sy[1:2]), 1.0)
    sb = jnp.where(valid, jnp.where(lane1 < 36, sx[2:3], sy[3:4]), 1.0)
    phi = p0[...] + p1[...] * sf
    psi = q0[...] + q1[...] * sb
    phi_before, phi_after = 1.0 - sf, va + vb * sf
    psi_after, psi_before = 1.0 - sb, ua + ub * sb
    wron = sf * psi_before + (ca + cb * sb) * phi_before
    inv_w = 1.0 / wron
    psi = psi * inv_w
    psi_after, psi_before = psi_after * inv_w, psi_before * inv_w
    phi_t, psi_t = phi.T, psi.T
    eps = ey[...]
    eps_t = rows_y[...]
    i0, j0 = iota((N, N), 0), iota((N, N), 1)
    low = i0 >= j0
    r8 = iota((8, N), 0)
    c8 = iota((8, N), 1)
    def from_either_end(pr, qr, ends):
        pb, pa, qb, qa = ends
        inv_p, inv_q = 1.0 / pr[:, N - 1 : N], 1.0 / qr[:, 0:1]
        beside = jnp.where(
            c8 == 0,
            pb * inv_p,
            jnp.where(c8 == 1, pa * inv_p, jnp.where(c8 == 2, qb * inv_q, qa * inv_q)),
        )
        return jnp.where(
            r8 == 0,
            pr * inv_p,
            jnp.where(r8 == 1, qr * inv_q, jnp.where(r8 == 2, beside, 0.0)),
        )

    for s in range(4):
        at = slice(32 + s, 33 + s)
        pr, qr, er = phi_t[at], psi_t[at], eps_t[at]
        pc, qc, ec = phi[:, at], psi[:, at], eps[:, at]
        ends = phi_before[:, at], phi_after[:, at], psi_before[:, at], psi_after[:, at]
        pb, pa, qb, qa = ends
        eq, ep = ec * qc, ec * pc
        gx[s] = jnp.where(low, eq * pr, ep * qr)
        lx[s] = jnp.where(j0 == 0, eq * pb, jnp.where(j0 == 1, ep * qa, 0.0))
        rx[s] = jnp.where(r8 == 0, pb * qr * er, jnp.where(r8 == 1, qa * pr * er, 0.0))
        hx[s] = from_either_end(pr, qr, ends)

        at = slice(36 + s, 37 + s)
        pr, qr, er = phi_t[at], psi_t[at], eps_t[at]
        pc, qc = phi[:, at], psi[:, at]
        ends = phi_before[:, at], phi_after[:, at], psi_before[:, at], psi_after[:, at]
        pb, pa, qb, qa = ends
        gy[s] = jnp.where(low, qc * (pr * er), pc * (qr * er))
        ry[s] = jnp.where(r8 == 0, pb * qr * er, jnp.where(r8 == 1, qa * pr * er, 0.0))
        hy[s] = from_either_end(pr, qr, ends)


def by_plane(ref, p, s, values):
    for z in range(4):
        q = 4 * s + z
        ref[p, q : q + 1, :] = values[:, z * N : (z + 1) * N]


def explicit(nx, ny, state, rate, hx, kin, cross, f_out, send, cells, cols, pay):
    k, l = lax.axis_index("row"), lax.axis_index("col")
    i0, j0 = iota((N, N), 0), iota((N, N), 1)
    for z in range(4):
        tiles, laps = [], []
        for s in range(4):
            t = state[s, z]
            xm = jnp.where(i0 == 0, 0.0, pltpu.roll(t, 1, 0))
            xp = jnp.where(i0 == N - 1, 0.0, pltpu.roll(t, N - 1, 0))
            ym = jnp.where(j0 == 0, 0.0, pltpu.roll(t, 1, 1))
            yp = jnp.where(j0 == N - 1, 0.0, pltpu.roll(t, N - 1, 1))
            tiles.append(t)
            laps.append(xm + xp + ym + yp - 4.0 * t)
        for j in range(4):
            react = (0.5 * kin[0, j]) * tiles[0]
            mix = (0.25 * cross[0, j]) * laps[0]
            for i in range(1, 4):
                react = react + (0.5 * kin[i, j]) * tiles[i]
                mix = mix + (0.25 * cross[i, j]) * laps[i]
            f_out[j, :, z * N : (z + 1) * N] = tiles[j] + rate[j, z] * react + mix

    side = jnp.zeros((N, N), f32)
    for s in range(4):
        for z in range(4):
            lane = 8 * s + 2 * z
            side = jnp.where(j0 == lane, state[s, z, :, 0:1], side)
            side = jnp.where(j0 == lane + 1, state[s, z, :, N - 1 : N], side)
    side = side.T
    r8, c8 = iota((8, N), 0), iota((8, N), 1)
    has = 0.25 * jnp.where(r8 % 2 == 0, (l > 0).astype(f32), (l < ny - 1).astype(f32))
    has_x = 0.25 * (k > 0).astype(f32), 0.25 * (k < nx - 1).astype(f32)
    tails = [jnp.zeros((8, N), f32)] * 2
    for j in range(4):
        mix = cross[0, j] * side[0:8]
        for i in range(1, 4):
            mix = mix + cross[i, j] * side[8 * i : 8 * i + 8]
        mix = has * mix
        cols[j] = mix
        beside = []
        for p, row in enumerate((0, N - 1)):
            pieces = []
            for z in range(4):
                piece = cross[0, j] * state[0, z, row : row + 1, :]
                for i in range(1, 4):
                    piece = piece + cross[i, j] * state[i, z, row : row + 1, :]
                pieces.append(has_x[p] * piece)
            beside.append(jnp.concatenate(pieces, axis=1))
            by_plane(cells, p, j, beside[p])
        sums = dot3(hx[j], f_out[j])
        for p in range(2):
            c = hx[j, 2:3, 2 * p : 2 * p + 1], hx[j, 2:3, 2 * p + 1 : 2 * p + 2]
            by_plane(pay, p, j, sums[p : p + 1] + c[0] * beside[0] + c[1] * beside[1])
            total = jnp.sum(mix * hx[j, p : p + 1, :], axis=1, keepdims=True)
            tails[p] = jnp.where(c8 == j, total, tails[p])
    for p in range(2):
        pay[p, 16:24, :] = tails[p]
    for j in range(nx):
        send[j] = pay[(j < k).astype(jnp.int32)]


def rows_kernel(
    nx, ny, f_in, cells, cols, recv, wx, wx_cols, gx, lx, rx, hy, g_out, send, beside, pay
):
    l = lax.axis_index("col")
    incoming = dot3(wx[...], recv[:, 0:16, :].reshape(nx * 16, N))
    from_before = incoming[0:16] + cells[0]
    from_after = incoming[16:32] + cells[1]
    in_cols = []
    for p in range(2):
        total = recv[0, 16:24, :] * wx_cols[p, 0:1, :]
        for j in range(1, nx):
            total = total + recv[j, 16:24, :] * wx_cols[p, j : j + 1, :]
        in_cols.append(total)
    for s in range(4):
        g = dot3(gx[s], f_in[s])
        lam, mu = lx[s, :, 0:1], lx[s, :, 1:2]
        col = (
            dot3(cols[s], gx[s], nt=True)
            + in_cols[0][:, s : s + 1] * rx[s, 0:1]
            + in_cols[1][:, s : s + 1] * rx[s, 1:2]
        )
        parts = []
        for z in range(4):
            q = slice(4 * s + z, 4 * s + z + 1)
            part = (
                g[:, z * N : (z + 1) * N] + lam * from_before[q] + mu * from_after[q]
            )
            g_out[s, z] = part
            parts.append(part)
        ends = dot3(hy[s], jnp.concatenate(parts, axis=0), nt=True)
        for p in range(2):
            c = hy[s, 2:3, 2 * p : 2 * p + 1], hy[s, 2:3, 2 * p + 1 : 2 * p + 2]
            for z in range(4):
                q = slice(4 * s + z, 4 * s + z + 1)
                before, after = col[2 * z : 2 * z + 1], col[2 * z + 1 : 2 * z + 2]
                pay[p, q, :] = (
                    ends[p : p + 1, z * N : (z + 1) * N] + c[0] * before + c[1] * after
                )
                beside[p, q, :] = after if p else before
    for m in range(ny):
        send[m] = pay[(m < l).astype(jnp.int32)]


def finish_cols(ny, g_in, recv, beside, wy, gy, ry, out, turned):
    incoming = dot3(wy[...], recv[...].reshape(ny * 16, N))
    turned[...] = jnp.concatenate(
        [
            incoming[0:16] + beside[0],
            incoming[16:32] + beside[1],
            jnp.zeros((N - 32, N), f32),
        ],
        axis=0,
    ).T
    for s in range(4):
        res = dot3(g_in[s].reshape(4 * N, N), gy[s])
        lam, mu = ry[s, 0:1], ry[s, 1:2]
        for z in range(4):
            q = 4 * s + z
            out[s, z] = (
                res[z * N : (z + 1) * N]
                + turned[:, q : q + 1] * lam
                + turned[:, 16 + q : 17 + q] * mu
            )


def next_kernel(
    nx, ny, g_in, recv, beside, wy, gy, ry, rate, hx, kin, cross,
    f_out, send, cells, cols, state, turned, pay,
):
    finish_cols(ny, g_in, recv, beside, wy, gy, ry, state, turned)
    explicit(nx, ny, state, rate, hx, kin, cross, f_out, send, cells, cols, pay)


def call(body, outs, scratch, smem=0, place=pltpu.VMEM):
    shapes = [jax.ShapeDtypeStruct(shape, f32) for shape in outs]

    def run(*args):
        count = len(args) - smem
        return pl.pallas_call(
            body,
            out_shape=shapes,
            in_specs=[pl.BlockSpec(memory_space=place)] * count
            + [pl.BlockSpec(memory_space=pltpu.SMEM)] * smem,
            out_specs=[pl.BlockSpec(memory_space=pltpu.VMEM)] * len(shapes),
            scratch_shapes=[
                pltpu.VMEM(shape, f32) if isinstance(shape, tuple) else shape
                for shape in scratch
            ],
            compiler_params=pltpu.CompilerParams(vmem_limit_bytes=VMEM),
            cost_estimate=pl.CostEstimate(
                flops=3_000_000_000, bytes_accessed=3_000_000, transcendentals=0
            ),
        )(*args)

    return run


def on_device(adjoint, rate_scale, kinetics, cross_matrix, x_diffusion, y_diffusion):
    nx, ny = lax.axis_size("row"), lax.axis_size("col")
    part = functools.partial
    gx, lx, rx, hx, gy, ry, hy, wx, wx_cols, wy = call(
        part(tables_kernel, nx, ny),
        [
            (4, N, N), (4, N, N), (4, 8, N), (4, 8, N), (4, N, N), (4, 8, N), (4, 8, N),
            (32, nx * 16), (2, nx, N), (32, ny * 16),
        ],
        [(N, N)] * 8 + [x_diffusion.shape, y_diffusion.shape, pltpu.SemaphoreType.DMA((2,))],
        place=pltpu.HBM,
    )(x_diffusion, y_diffusion)
    tile = (4, 4, N, N)
    step_out = [(4, N, 4 * N), (nx, 24, N), (2, 16, N), (4, 8, N)]
    f, send, cells, cols = call(part(explicit, nx, ny), step_out, [(2, 24, N)], 2)(
        adjoint, rate_scale, hx, kinetics, cross_matrix
    )
    for step in range(STEPS):
        recv = lax.all_to_all(send, "row", 0, 0, tiled=True)
        g, send, beside = call(
            part(rows_kernel, nx, ny), [tile, (ny, 16, N), (2, 16, N)], [(2, 16, N)]
        )(f, cells, cols, recv, wx, wx_cols, gx, lx, rx, hy)
        recv = lax.all_to_all(send, "col", 0, 0, tiled=True)
        if step + 1 < STEPS:
            f, send, cells, cols = call(
                part(next_kernel, nx, ny), step_out, [tile, (N, N), (2, 24, N)], 2
            )(g, recv, beside, wy, gy, ry, rate_scale, hx, kinetics, cross_matrix)
    (out,) = call(part(finish_cols, ny), [tile], [(N, N)])(g, recv, beside, wy, gy, ry)
    return out


def solution(mesh):
    return jax.shard_map(
        on_device,
        mesh=mesh,
        in_specs=(P(None, None, "row", "col"), P(None, None, "row", "col"), P(), P(), P(), P()),
        out_specs=P(None, None, "row", "col"),
        check_vma=False,
    )
```

```python
import functools

import jax
import jax.numpy as jnp
from jax import lax
from jax.experimental import pallas as pl
from jax.experimental.pallas import tpu as pltpu
from jax.sharding import PartitionSpec as P

M = 1000.0
STEPS = 2
N = 128
STRIP = 32
f32 = jnp.float32
bf16 = jnp.bfloat16
VMEM = 20 * 1024 * 1024


def iota(shape, dim):
    return lax.broadcasted_iota(jnp.int32, shape, dim)


def split(a):
    hi = a.astype(bf16).astype(f32)
    return hi, a - hi


def bdot(a, b, nt=False):
    dims = (((1,), (1 if nt else 0,)), ((), ()))
    return lax.dot_general(
        a.astype(bf16), b.astype(bf16), dims, preferred_element_type=f32
    )


def dot_rows(a, b, nt=False):
    ah, al = split(a)
    bh, bl = split(b)
    n = a.shape[0]
    left = jnp.concatenate(
        [jnp.concatenate([ah, ah], axis=1), jnp.concatenate([al, al], axis=1)], axis=0
    )
    out = bdot(left, jnp.concatenate([bh, bl], axis=1 if nt else 0), nt)
    return out[0:n] + out[n:]


def dot_cols(a, b):
    ah, al = split(a)
    bh, bl = split(b)
    n = b.shape[1]
    right = jnp.concatenate([bh, bl], axis=1)
    out = bdot(
        jnp.concatenate([ah, al], axis=1), jnp.concatenate([right, right], axis=0)
    )
    return out[:, 0:n] + out[:, n:]


def dot_mixed(a, b):
    ah, al = split(a)
    bh, bl = split(b)
    m, n = a.shape[0], b.shape[1]
    out = bdot(jnp.concatenate([ah, al], axis=0), jnp.concatenate([bh, bl], axis=1))
    return (out[0:m, 0:n] + out[m:, n:]) + (out[0:m, n:] + out[m:, 0:n])


def pick(a, hit):
    hi, rest = split(a)
    mid, low = split(rest)
    n = a.shape[0]
    out = bdot(jnp.concatenate([hi, mid, low], axis=0), jnp.where(hit, 1.0, 0.0))
    return (out[0:n] + out[n : 2 * n]) + out[2 * n :]


def tables_kernel(
    nx, ny, eps_all, gx, lx, rx, hx, gy, ry, hy, wx, wx_cols, wy,
    rows_x, rows_y, ex, ey, p0, p1, q0, q1,
):
    k = lax.axis_index("row")
    l = lax.axis_index("col")
    rows_x[...] = jnp.full((N, N), 1.0 / M, f32)
    rows_y[...] = jnp.full((N, N), 1.0 / M, f32)
    for j in range(nx):
        rows_x[4 * j : 4 * j + 4, :] = eps_all[:, j * N : (j + 1) * N]
    for j in range(ny):
        rows_y[4 * j : 4 * j + 4, :] = eps_all[:, (nx + j) * N : (nx + j + 1) * N]

    def block(index):
        return eps_all[:, pl.ds(pl.multiple_of(index * N, N), N)]

    rows_y[32:36, :] = block(k)
    rows_y[36:40, :] = block(nx + l)
    ex[...] = rows_x[...].T
    ey[...] = rows_y[...].T

    first2 = (iota((2, N), 0) == 0).astype(f32)
    one, zero = jnp.ones((1, N), f32), jnp.zeros((1, N), f32)

    def advance(e, v, d):
        grown = e * v
        return (v + d) + grown, d + grown

    def body(i, carry):
        vx, dx, va, da, vb, db, ux, cx, ua, ca, ub, cb = carry
        at = pl.multiple_of(i * 8, 8)
        back = pl.multiple_of(N - 8 - i * 8, 8)
        ex_f, ey_f = ex[pl.ds(at, 8), :], ey[pl.ds(at, 8), :]
        ex_b, ey_b = ex[pl.ds(back, 8), :], ey[pl.ds(back, 8), :]
        for r in range(8):
            t = at + r
            p0[pl.ds(t, 1), :] = va
            p1[pl.ds(t, 1), :] = vb
            e, ee = ex_f[r : r + 1], ey_f[r : r + 1]
            vx, dx = advance(e, vx, dx)
            va, da = advance(ee, va, da)
            vb, db = advance(ee, vb, db)
            r2 = 7 - r
            t = back + r2
            q0[pl.ds(t, 1), :] = ua
            q1[pl.ds(t, 1), :] = ub
            e, ee = ex_b[r2 : r2 + 1], ey_b[r2 : r2 + 1]
            ux, cx = advance(e, ux, cx)
            ua, ca = advance(ee, ua, ca)
            ub, cb = advance(ee, ub, cb)
        return vx, dx, va, da, vb, db, ux, cx, ua, ca, ub, cb

    init = (first2, 1.0 - first2, one, zero, zero, one)
    vx, dx, va, da, vb, db, ux, cx, ua, ca, ub, cb = lax.fori_loop(
        0, N // 8, body, init + init
    )

    row = iota((8, N), 0)
    lane = iota((8, N), 1)
    blk = lane // 4
    forward = row < 2
    is_x = row % 2 == 0
    count = jnp.where(is_x, nx, ny)
    own = jnp.where(is_x, k, l)
    place = jnp.where(forward, blk, count - 1 - blk)
    own = jnp.where(forward, own, count - 1 - own)

    def pack(a, b, c, d):
        return jnp.where(
            row == 0, a, jnp.where(row == 1, b, jnp.where(row == 2, c, d))
        )

    def shifted(a, by):
        return jnp.where(
            forward, pltpu.roll(a, 4 * by, 1), pltpu.roll(a, N - 4 * by, 1)
        )

    def outside(by):
        return place < by

    a0 = pack(vx[0:1], va, ux[0:1], ua)
    b0 = pack(vx[1:2], vb, ux[1:2], ub)
    c0 = pack(dx[0:1], da, cx[0:1], ca)
    d0 = pack(dx[1:2], db, cx[1:2], cb)
    a, b, c, d = a0, b0, c0, d0
    by = 1
    while by < max(nx, ny):
        skip = outside(by)
        sa = jnp.where(skip, 1.0, shifted(a, by))
        sb = jnp.where(skip, 0.0, shifted(b, by))
        sc = jnp.where(skip, 0.0, shifted(c, by))
        sd = jnp.where(skip, 1.0, shifted(d, by))
        a, b, c, d = a * sa + b * sc, a * sb + b * sd, c * sa + d * sc, c * sb + d * sd
        by *= 2
        if by == 16:
            norm = 1.0 / (a + b)
            a, b, c, d = a * norm, b * norm, c * norm, d * norm
    skip = outside(1)
    slope = jnp.where(skip, 1.0, shifted((c + d) / (a + b), 1))

    decay = (1.0 - slope) / ((a0 + b0 * slope) - (c0 + d0 * slope))
    between = (place < own) & (place >= 0)
    prod = jnp.where(between, decay, 1.0)

    def against(a, by):
        return jnp.where(
            forward, pltpu.roll(a, N - 4 * by, 1), pltpu.roll(a, 4 * by, 1)
        )

    def past(by):
        return place + by >= count

    by = 1
    while by < max(nx, ny):
        prod = prod * jnp.where(past(by), 1.0, against(prod, by))
        by *= 2
    weight = jnp.where(between, jnp.where(past(1), 1.0, against(prod, 1)), 0.0)

    def expand(width, per_block, species_of):
        src = iota((N, width), 0)
        col = iota((N, width), 1)
        hit = (src // 4 == col // per_block) & (src % 4 == species_of(col % per_block))
        return pick(weight, hit)

    width = nx * 16
    spread = expand(width, 16, lambda r: r // 4)
    rr, cc = iota((32, width), 0), iota((32, width), 1)
    wx[...] = jnp.where(
        rr % 16 == cc % 16, jnp.where(rr < 16, spread[0:1], spread[2:3]), 0.0
    )
    own_lanes = iota((nx, N), 1) // 4 == iota((nx, N), 0)
    by_species = iota((N, N), 0) % 4 == iota((N, N), 1)
    for p in range(2):
        wx_cols[p] = pick(
            jnp.where(own_lanes, weight[2 * p : 2 * p + 1], 0.0), by_species
        )
    width = ny * 16
    spread = expand(width, 16, lambda r: r // 4)
    rr, cc = iota((32, width), 0), iota((32, width), 1)
    wy[...] = jnp.where(
        rr % 16 == cc % 16, jnp.where(rr < 16, spread[1:2], spread[3:4]), 0.0
    )

    lane1 = iota((1, N), 1)
    to_x = lax.rem(32 - 4 * k + N, N)
    to_y = lax.rem(36 - 4 * l + N, N)
    sx = pltpu.roll(slope, to_x, 1)
    sy = pltpu.roll(slope, to_y, 1)
    valid = (lane1 >= 32) & (lane1 < 40)
    sf = jnp.where(valid, jnp.where(lane1 < 36, sx[0:1], sy[1:2]), 1.0)
    sb = jnp.where(valid, jnp.where(lane1 < 36, sx[2:3], sy[3:4]), 1.0)
    phi = p0[...] + p1[...] * sf
    psi = q0[...] + q1[...] * sb
    phi_before, phi_after = 1.0 - sf, va + vb * sf
    psi_after, psi_before = 1.0 - sb, ua + ub * sb
    wron = sf * psi_before + (ca + cb * sb) * phi_before
    inv_w = 1.0 / wron
    psi = psi * inv_w
    psi_after, psi_before = psi_after * inv_w, psi_before * inv_w
    phi_t, psi_t = phi.T, psi.T
    eps = ey[...]
    eps_t = rows_y[...]
    i0, j0 = iota((N, N), 0), iota((N, N), 1)
    low = i0 >= j0
    r8 = iota((8, N), 0)
    c8 = iota((8, N), 1)
    def from_either_end(pr, qr, ends):
        pb, pa, qb, qa = ends
        inv_p, inv_q = 1.0 / pr[:, N - 1 : N], 1.0 / qr[:, 0:1]
        beside = jnp.where(
            c8 == 0,
            pb * inv_p,
            jnp.where(c8 == 1, pa * inv_p, jnp.where(c8 == 2, qb * inv_q, qa * inv_q)),
        )
        return jnp.where(
            r8 == 0,
            pr * inv_p,
            jnp.where(r8 == 1, qr * inv_q, jnp.where(r8 == 2, beside, 0.0)),
        )

    for s in range(4):
        at = slice(32 + s, 33 + s)
        pr, qr, er = phi_t[at], psi_t[at], eps_t[at]
        pc, qc, ec = phi[:, at], psi[:, at], eps[:, at]
        ends = phi_before[:, at], phi_after[:, at], psi_before[:, at], psi_after[:, at]
        pb, pa, qb, qa = ends
        eq, ep = ec * qc, ec * pc
        gx[s] = jnp.where(low, eq * pr, ep * qr)
        lx[s] = jnp.where(j0 == 0, eq * pb, jnp.where(j0 == 1, ep * qa, 0.0))
        rx[s] = jnp.where(r8 == 0, pb * qr * er, jnp.where(r8 == 1, qa * pr * er, 0.0))
        hx[s] = from_either_end(pr, qr, ends)

        at = slice(36 + s, 37 + s)
        pr, qr, er = phi_t[at], psi_t[at], eps_t[at]
        pc, qc = phi[:, at], psi[:, at]
        ends = phi_before[:, at], phi_after[:, at], psi_before[:, at], psi_after[:, at]
        pb, pa, qb, qa = ends
        gy[s] = jnp.where(low, qc * (pr * er), pc * (qr * er))
        ry[s] = jnp.where(r8 == 0, pb * qr * er, jnp.where(r8 == 1, qa * pr * er, 0.0))
        hy[s] = from_either_end(pr, qr, ends)


def by_plane(ref, p, s, values):
    for z in range(4):
        q = 4 * s + z
        ref[p, q : q + 1, :] = values[:, z * N : (z + 1) * N]


def explicit(nx, ny, state, rate, hx, kin, cross, f_out, send, cells, cols, pay):
    k, l = lax.axis_index("row"), lax.axis_index("col")
    j0 = iota((N, N), 1)
    ri, rj = iota((STRIP, N), 0), iota((STRIP, N), 1)
    for z in range(4):
        for at in range(0, N, STRIP):
            end = at + STRIP
            tiles, laps = [], []
            for s in range(4):
                t = state[s, z, at:end, :]
                if at == 0:
                    xm = jnp.where(ri == 0, 0.0, pltpu.roll(t, 1, 0))
                else:
                    xm = state[s, z, at - 1 : end - 1, :]
                if end == N:
                    xp = jnp.where(ri == STRIP - 1, 0.0, pltpu.roll(t, STRIP - 1, 0))
                else:
                    xp = state[s, z, at + 1 : end + 1, :]
                ym = jnp.where(rj == 0, 0.0, pltpu.roll(t, 1, 1))
                yp = jnp.where(rj == N - 1, 0.0, pltpu.roll(t, N - 1, 1))
                tiles.append(t)
                laps.append(xm + xp + ym + yp - 4.0 * t)
            for j in range(4):
                react = (0.5 * kin[0, j]) * tiles[0]
                mix = (0.25 * cross[0, j]) * laps[0]
                for i in range(1, 4):
                    react = react + (0.5 * kin[i, j]) * tiles[i]
                    mix = mix + (0.25 * cross[i, j]) * laps[i]
                f_out[j, at:end, z * N : (z + 1) * N] = (
                    tiles[j] + rate[j, z, at:end, :] * react + mix
                )

    side = jnp.zeros((N, N), f32)
    for s in range(4):
        for z in range(4):
            q = 4 * s + z
            side = jnp.where(j0 // 2 == q, pltpu.roll(state[s, z], 2 * q + 1, 1), side)
    side = side.T
    r8, c8 = iota((8, N), 0), iota((8, N), 1)
    has = 0.25 * jnp.where(r8 % 2 == 0, (l < ny - 1).astype(f32), (l > 0).astype(f32))
    has_x = 0.25 * (k > 0).astype(f32), 0.25 * (k < nx - 1).astype(f32)
    tails = [jnp.zeros((8, N), f32)] * 2
    for j in range(4):
        mix = cross[0, j] * side[0:8]
        for i in range(1, 4):
            mix = mix + cross[i, j] * side[8 * i : 8 * i + 8]
        mix = has * mix
        cols[j] = mix
        beside = []
        for p, row in enumerate((0, N - 1)):
            pieces = []
            for z in range(4):
                piece = cross[0, j] * state[0, z, row : row + 1, :]
                for i in range(1, 4):
                    piece = piece + cross[i, j] * state[i, z, row : row + 1, :]
                pieces.append(has_x[p] * piece)
            beside.append(jnp.concatenate(pieces, axis=1))
            by_plane(cells, p, j, beside[p])
        sums = dot_rows(hx[j], f_out[j])
        for p in range(2):
            c = hx[j, 2:3, 2 * p : 2 * p + 1], hx[j, 2:3, 2 * p + 1 : 2 * p + 2]
            by_plane(pay, p, j, sums[p : p + 1] + c[0] * beside[0] + c[1] * beside[1])
            total = jnp.sum(mix * hx[j, p : p + 1, :], axis=1, keepdims=True)
            tails[p] = jnp.where(c8 == j, total, tails[p])
    for p in range(2):
        pay[p, 16:24, :] = tails[p]
    for j in range(nx):
        send[j] = pay[(j < k).astype(jnp.int32)]


def rows_kernel(
    nx, ny, f_in, cells, cols, recv, wx, wx_cols, gx, lx, rx, hy, g_out, send, beside, pay
):
    l = lax.axis_index("col")
    incoming = dot_mixed(wx[...], recv[:, 0:16, :].reshape(nx * 16, N))
    from_before = incoming[0:16] + cells[0]
    from_after = incoming[16:32] + cells[1]
    in_cols = []
    for p in range(2):
        total = recv[0, 16:24, :] * wx_cols[p, 0:1, :]
        for j in range(1, nx):
            total = total + recv[j, 16:24, :] * wx_cols[p, j : j + 1, :]
        in_cols.append(total)
    for s in range(4):
        g = dot_rows(gx[s], f_in[s])
        lam, mu = lx[s, :, 0:1], lx[s, :, 1:2]
        col = (
            dot_rows(cols[s], gx[s], nt=True)
            + in_cols[0][:, s : s + 1] * rx[s, 0:1]
            + in_cols[1][:, s : s + 1] * rx[s, 1:2]
        )
        parts = []
        for z in range(4):
            q = slice(4 * s + z, 4 * s + z + 1)
            part = (
                g[:, z * N : (z + 1) * N] + lam * from_before[q] + mu * from_after[q]
            )
            g_out[s, z] = part
            parts.append(part)
        ends = dot_rows(hy[s], jnp.concatenate(parts, axis=0), nt=True)
        for p in range(2):
            c = hy[s, 2:3, 2 * p : 2 * p + 1], hy[s, 2:3, 2 * p + 1 : 2 * p + 2]
            for z in range(4):
                q = slice(4 * s + z, 4 * s + z + 1)
                after, before = col[2 * z : 2 * z + 1], col[2 * z + 1 : 2 * z + 2]
                pay[p, q, :] = (
                    ends[p : p + 1, z * N : (z + 1) * N] + c[0] * before + c[1] * after
                )
                beside[p, q, :] = after if p else before
    for m in range(ny):
        send[m] = pay[(m < l).astype(jnp.int32)]


def finish_cols(ny, g_in, recv, beside, wy, gy, ry, out, turned, done=None):
    incoming = dot_mixed(wy[...], recv[...].reshape(ny * 16, N))
    turned[...] = jnp.concatenate(
        [
            incoming[0:16] + beside[0],
            incoming[16:32] + beside[1],
            jnp.zeros((N - 32, N), f32),
        ],
        axis=0,
    ).T
    for s in range(4):
        res = dot_cols(g_in[s].reshape(4 * N, N), gy[s])
        lam, mu = ry[s, 0:1], ry[s, 1:2]
        for z in range(4):
            q = 4 * s + z
            out[s, z] = (
                res[z * N : (z + 1) * N]
                + turned[:, q : q + 1] * lam
                + turned[:, 16 + q : 17 + q] * mu
            )
        if done is not None:
            done(s)


def last_kernel(ny, g_in, recv, beside, wy, gy, ry, out, state, turned, sent):
    copies = [
        pltpu.make_async_copy(state.at[s], out.at[s], sent.at[s]) for s in range(4)
    ]
    finish_cols(
        ny, g_in, recv, beside, wy, gy, ry, state, turned, lambda s: copies[s].start()
    )
    for copy in copies:
        copy.wait()


def next_kernel(
    nx, ny, g_in, recv, beside, wy, gy, ry, rate, hx, kin, cross,
    f_out, send, cells, cols, state, turned, pay,
):
    finish_cols(ny, g_in, recv, beside, wy, gy, ry, state, turned)
    explicit(nx, ny, state, rate, hx, kin, cross, f_out, send, cells, cols, pay)


def call(body, outs, scratch, smem=0, place_out=pltpu.VMEM):
    shapes = [jax.ShapeDtypeStruct(shape, f32) for shape in outs]

    def run(*args):
        count = len(args) - smem
        return pl.pallas_call(
            body,
            out_shape=shapes,
            in_specs=[pl.BlockSpec(memory_space=pltpu.VMEM)] * count
            + [pl.BlockSpec(memory_space=pltpu.SMEM)] * smem,
            out_specs=[pl.BlockSpec(memory_space=place_out)] * len(shapes),
            scratch_shapes=[
                pltpu.VMEM(shape, f32) if isinstance(shape, tuple) else shape
                for shape in scratch
            ],
            compiler_params=pltpu.CompilerParams(vmem_limit_bytes=VMEM),
            cost_estimate=pl.CostEstimate(
                flops=3_000_000_000, bytes_accessed=3_000_000, transcendentals=0
            ),
        )(*args)

    return run


def on_device(adjoint, rate_scale, kinetics, cross_matrix, x_diffusion, y_diffusion):
    nx, ny = lax.axis_size("row"), lax.axis_size("col")
    part = functools.partial
    gx, lx, rx, hx, gy, ry, hy, wx, wx_cols, wy = call(
        part(tables_kernel, nx, ny),
        [
            (4, N, N), (4, N, N), (4, 8, N), (4, 8, N), (4, N, N), (4, 8, N), (4, 8, N),
            (32, nx * 16), (2, nx, N), (32, ny * 16),
        ],
        [(N, N)] * 8,
    )(1.0 / (M * jnp.concatenate([x_diffusion, y_diffusion], axis=1)))
    tile = (4, 4, N, N)
    step_out = [(4, N, 4 * N), (nx, 24, N), (2, 16, N), (4, 8, N)]
    f, send, cells, cols = call(part(explicit, nx, ny), step_out, [(2, 24, N)], 2)(
        adjoint, rate_scale, hx, kinetics, cross_matrix
    )
    for step in range(STEPS):
        recv = lax.all_to_all(send, "row", 0, 0, tiled=True)
        g, send, beside = call(
            part(rows_kernel, nx, ny), [tile, (ny, 16, N), (2, 16, N)], [(2, 16, N)]
        )(f, cells, cols, recv, wx, wx_cols, gx, lx, rx, hy)
        recv = lax.all_to_all(send, "col", 0, 0, tiled=True)
        if step + 1 < STEPS:
            f, send, cells, cols = call(
                part(next_kernel, nx, ny), step_out, [tile, (N, N), (2, 24, N)], 2
            )(g, recv, beside, wy, gy, ry, rate_scale, hx, kinetics, cross_matrix)
    (out,) = call(
        part(last_kernel, ny),
        [tile],
        [tile, (N, N), pltpu.SemaphoreType.DMA((4,))],
        place_out=pl.ANY,
    )(g, recv, beside, wy, gy, ry)
    return out


def solution(mesh):
    return jax.shard_map(
        on_device,
        mesh=mesh,
        in_specs=(P(None, None, "row", "col"), P(None, None, "row", "col"), P(), P(), P(), P()),
        out_specs=P(None, None, "row", "col"),
        check_vma=False,
    )
```

```python
import functools

import jax
import jax.numpy as jnp
from jax import lax
from jax.experimental import pallas as pl
from jax.experimental.pallas import tpu as pltpu
from jax.sharding import PartitionSpec as P

M = 1000.0
STEPS = 2
N = 128
STRIP = 32
f32 = jnp.float32
bf16 = jnp.bfloat16
VMEM = 20 * 1024 * 1024


def iota(shape, dim):
    return lax.broadcasted_iota(jnp.int32, shape, dim)


def split(a):
    hi = a.astype(bf16).astype(f32)
    return hi, a - hi


def bdot(a, b, nt=False):
    dims = (((1,), (1 if nt else 0,)), ((), ()))
    return lax.dot_general(
        a.astype(bf16), b.astype(bf16), dims, preferred_element_type=f32
    )


def dot_rows(a, b, nt=False):
    ah, al = split(a)
    bh, bl = split(b)
    n = a.shape[0]
    left = jnp.concatenate(
        [jnp.concatenate([ah, ah], axis=1), jnp.concatenate([al, al], axis=1)], axis=0
    )
    out = bdot(left, jnp.concatenate([bh, bl], axis=1 if nt else 0), nt)
    return out[0:n] + out[n:]


def dot_cols(a, b):
    ah, al = split(a)
    bh, bl = split(b)
    n = b.shape[1]
    right = jnp.concatenate([bh, bl], axis=1)
    out = bdot(
        jnp.concatenate([ah, al], axis=1), jnp.concatenate([right, right], axis=0)
    )
    return out[:, 0:n] + out[:, n:]


def dot_mixed(a, b):
    ah, al = split(a)
    bh, bl = split(b)
    m, n = a.shape[0], b.shape[1]
    out = bdot(jnp.concatenate([ah, al], axis=0), jnp.concatenate([bh, bl], axis=1))
    return (out[0:m, 0:n] + out[m:, n:]) + (out[0:m, n:] + out[m:, 0:n])


def pick(a, hit):
    hi, rest = split(a)
    mid, low = split(rest)
    n = a.shape[0]
    out = bdot(jnp.concatenate([hi, mid, low], axis=0), jnp.where(hit, 1.0, 0.0))
    return (out[0:n] + out[n : 2 * n]) + out[2 * n :]


def tables_kernel(
    nx, ny, eps_all, gx, lx, rx, hx, gy, ry, hy, wx, wx_cols, wy,
    rows_x, rows_y, ex, ey, p0, p1, q0, q1,
):
    k = lax.axis_index("row")
    l = lax.axis_index("col")
    rows_x[...] = jnp.full((N, N), 1.0 / M, f32)
    rows_y[...] = jnp.full((N, N), 1.0 / M, f32)
    for j in range(nx):
        rows_x[4 * j : 4 * j + 4, :] = eps_all[:, j * N : (j + 1) * N]
    for j in range(ny):
        rows_y[4 * j : 4 * j + 4, :] = eps_all[:, (nx + j) * N : (nx + j + 1) * N]

    def block(index):
        return eps_all[:, pl.ds(pl.multiple_of(index * N, N), N)]

    rows_y[32:36, :] = block(k)
    rows_y[36:40, :] = block(nx + l)
    ex[...] = rows_x[...].T
    ey[...] = rows_y[...].T

    first2 = (iota((2, N), 0) == 0).astype(f32)
    one, zero = jnp.ones((1, N), f32), jnp.zeros((1, N), f32)

    def advance(e, v, d):
        grown = e * v
        return (v + d) + grown, d + grown

    def body(i, carry):
        vx, dx, va, da, vb, db, ux, cx, ua, ca, ub, cb = carry
        at = pl.multiple_of(i * 8, 8)
        back = pl.multiple_of(N - 8 - i * 8, 8)
        ex_f, ey_f = ex[pl.ds(at, 8), :], ey[pl.ds(at, 8), :]
        ex_b, ey_b = ex[pl.ds(back, 8), :], ey[pl.ds(back, 8), :]
        for r in range(8):
            t = at + r
            p0[pl.ds(t, 1), :] = va
            p1[pl.ds(t, 1), :] = vb
            e, ee = ex_f[r : r + 1], ey_f[r : r + 1]
            vx, dx = advance(e, vx, dx)
            va, da = advance(ee, va, da)
            vb, db = advance(ee, vb, db)
            r2 = 7 - r
            t = back + r2
            q0[pl.ds(t, 1), :] = ua
            q1[pl.ds(t, 1), :] = ub
            e, ee = ex_b[r2 : r2 + 1], ey_b[r2 : r2 + 1]
            ux, cx = advance(e, ux, cx)
            ua, ca = advance(ee, ua, ca)
            ub, cb = advance(ee, ub, cb)
        return vx, dx, va, da, vb, db, ux, cx, ua, ca, ub, cb

    init = (first2, 1.0 - first2, one, zero, zero, one)
    vx, dx, va, da, vb, db, ux, cx, ua, ca, ub, cb = lax.fori_loop(
        0, N // 8, body, init + init
    )

    row = iota((8, N), 0)
    lane = iota((8, N), 1)
    blk = lane // 4
    forward = row < 2
    is_x = row % 2 == 0
    count = jnp.where(is_x, nx, ny)
    own = jnp.where(is_x, k, l)
    place = jnp.where(forward, blk, count - 1 - blk)
    own = jnp.where(forward, own, count - 1 - own)

    def pack(a, b, c, d):
        return jnp.where(
            row == 0, a, jnp.where(row == 1, b, jnp.where(row == 2, c, d))
        )

    def shifted(a, by):
        return jnp.where(
            forward, pltpu.roll(a, 4 * by, 1), pltpu.roll(a, N - 4 * by, 1)
        )

    def outside(by):
        return place < by

    a0 = pack(vx[0:1], va, ux[0:1], ua)
    b0 = pack(vx[1:2], vb, ux[1:2], ub)
    c0 = pack(dx[0:1], da, cx[0:1], ca)
    d0 = pack(dx[1:2], db, cx[1:2], cb)
    a, b, c, d = a0, b0, c0, d0
    by = 1
    while by < max(nx, ny):
        skip = outside(by)
        sa = jnp.where(skip, 1.0, shifted(a, by))
        sb = jnp.where(skip, 0.0, shifted(b, by))
        sc = jnp.where(skip, 0.0, shifted(c, by))
        sd = jnp.where(skip, 1.0, shifted(d, by))
        a, b, c, d = a * sa + b * sc, a * sb + b * sd, c * sa + d * sc, c * sb + d * sd
        by *= 2
        if by == 16:
            norm = 1.0 / (a + b)
            a, b, c, d = a * norm, b * norm, c * norm, d * norm
    skip = outside(1)
    slope = jnp.where(skip, 1.0, shifted((c + d) / (a + b), 1))

    decay = (1.0 - slope) / ((a0 + b0 * slope) - (c0 + d0 * slope))
    between = (place < own) & (place >= 0)
    prod = jnp.where(between, decay, 1.0)

    def against(a, by):
        return jnp.where(
            forward, pltpu.roll(a, N - 4 * by, 1), pltpu.roll(a, 4 * by, 1)
        )

    def past(by):
        return place + by >= count

    by = 1
    while by < max(nx, ny):
        prod = prod * jnp.where(past(by), 1.0, against(prod, by))
        by *= 2
    weight = jnp.where(between, jnp.where(past(1), 1.0, against(prod, 1)), 0.0)

    def expand(width, per_block, species_of):
        src = iota((N, width), 0)
        col = iota((N, width), 1)
        hit = (src // 4 == col // per_block) & (src % 4 == species_of(col % per_block))
        return pick(weight, hit)

    width = nx * 16
    spread = expand(width, 16, lambda r: r // 4)
    rr, cc = iota((32, width), 0), iota((32, width), 1)
    wx[...] = jnp.where(
        rr % 16 == cc % 16, jnp.where(rr < 16, spread[0:1], spread[2:3]), 0.0
    )
    own_lanes = iota((nx, N), 1) // 4 == iota((nx, N), 0)
    by_species = iota((N, N), 0) % 4 == iota((N, N), 1)
    for p in range(2):
        wx_cols[p] = pick(
            jnp.where(own_lanes, weight[2 * p : 2 * p + 1], 0.0), by_species
        )
    width = ny * 16
    spread = expand(width, 16, lambda r: r // 4)
    rr, cc = iota((32, width), 0), iota((32, width), 1)
    wy[...] = jnp.where(
        rr % 16 == cc % 16, jnp.where(rr < 16, spread[1:2], spread[3:4]), 0.0
    )

    lane1 = iota((1, N), 1)
    to_x = lax.rem(32 - 4 * k + N, N)
    to_y = lax.rem(36 - 4 * l + N, N)
    sx = pltpu.roll(slope, to_x, 1)
    sy = pltpu.roll(slope, to_y, 1)
    valid = (lane1 >= 32) & (lane1 < 40)
    sf = jnp.where(valid, jnp.where(lane1 < 36, sx[0:1], sy[1:2]), 1.0)
    sb = jnp.where(valid, jnp.where(lane1 < 36, sx[2:3], sy[3:4]), 1.0)
    phi = p0[...] + p1[...] * sf
    psi = q0[...] + q1[...] * sb
    phi_before, phi_after = 1.0 - sf, va + vb * sf
    psi_after, psi_before = 1.0 - sb, ua + ub * sb
    wron = sf * psi_before + (ca + cb * sb) * phi_before
    inv_w = 1.0 / wron
    psi = psi * inv_w
    psi_after, psi_before = psi_after * inv_w, psi_before * inv_w
    phi_t, psi_t = phi.T, psi.T
    eps = ey[...]
    eps_t = rows_y[...]
    i0, j0 = iota((N, N), 0), iota((N, N), 1)
    low = i0 >= j0
    r8 = iota((8, N), 0)
    c8 = iota((8, N), 1)
    def from_either_end(pr, qr, ends):
        pb, pa, qb, qa = ends
        inv_p, inv_q = 1.0 / pr[:, N - 1 : N], 1.0 / qr[:, 0:1]
        beside = jnp.where(
            c8 == 0,
            pb * inv_p,
            jnp.where(c8 == 1, pa * inv_p, jnp.where(c8 == 2, qb * inv_q, qa * inv_q)),
        )
        return jnp.where(
            r8 == 0,
            pr * inv_p,
            jnp.where(r8 == 1, qr * inv_q, jnp.where(r8 == 2, beside, 0.0)),
        )

    wide = iota((N, 4 * N), 0)
    line, plane = wide % 16, iota((N, 4 * N), 1) // N
    from_after, high = (wide // 16) % 2 == 1, wide < 64

    for s in range(4):
        at = slice(32 + s, 33 + s)
        pr, qr, er = phi_t[at], psi_t[at], eps_t[at]
        pc, qc, ec = phi[:, at], psi[:, at], eps[:, at]
        ends = phi_before[:, at], phi_after[:, at], psi_before[:, at], psi_after[:, at]
        pb, pa, qb, qa = ends
        eq, ep = ec * qc, ec * pc
        gx[s] = jnp.where(low, eq * pr, ep * qr)
        lx[s] = jnp.where(j0 == 0, eq * pb, jnp.where(j0 == 1, ep * qa, 0.0))
        rx[s] = jnp.where(r8 == 0, pb * qr * er, jnp.where(r8 == 1, qa * pr * er, 0.0))
        hx[s] = from_either_end(pr, qr, ends)

        at = slice(36 + s, 37 + s)
        pr, qr, er = phi_t[at], psi_t[at], eps_t[at]
        pc, qc = phi[:, at], psi[:, at]
        ends = phi_before[:, at], phi_after[:, at], psi_before[:, at], psi_after[:, at]
        pb, pa, qb, qa = ends
        gy[s] = jnp.where(low, qc * (pr * er), pc * (qr * er))
        lam, mu = split(pb * qr * er), split(qa * pr * er)
        part = [
            jnp.where(from_after, jnp.concatenate([m] * 4, 1), jnp.concatenate([v] * 4, 1))
            for v, m in zip(lam, mu)
        ]
        ry[s] = jnp.where(
            line == 4 * s + plane, jnp.where(high, part[0], part[1]), 0.0
        ).astype(bf16)
        hy[s] = from_either_end(pr, qr, ends)


def by_plane(ref, p, s, values):
    for z in range(4):
        q = 4 * s + z
        ref[p, q : q + 1, :] = values[:, z * N : (z + 1) * N]


def explicit(nx, ny, state, rate, hx, kin, cross, f_out, send, cells, cols, pay):
    k, l = lax.axis_index("row"), lax.axis_index("col")
    j0 = iota((N, N), 1)
    ri, rj = iota((STRIP, N), 0), iota((STRIP, N), 1)
    for z in range(4):
        for at in range(0, N, STRIP):
            end = at + STRIP
            tiles, laps = [], []
            for s in range(4):
                t = state[s, z, at:end, :]
                if at == 0:
                    xm = jnp.where(ri == 0, 0.0, pltpu.roll(t, 1, 0))
                else:
                    xm = state[s, z, at - 1 : end - 1, :]
                if end == N:
                    xp = jnp.where(ri == STRIP - 1, 0.0, pltpu.roll(t, STRIP - 1, 0))
                else:
                    xp = state[s, z, at + 1 : end + 1, :]
                ym = jnp.where(rj == 0, 0.0, pltpu.roll(t, 1, 1))
                yp = jnp.where(rj == N - 1, 0.0, pltpu.roll(t, N - 1, 1))
                tiles.append(t)
                laps.append(xm + xp + ym + yp - 4.0 * t)
            for j in range(4):
                react = (0.5 * kin[0, j]) * tiles[0]
                mix = (0.25 * cross[0, j]) * laps[0]
                for i in range(1, 4):
                    react = react + (0.5 * kin[i, j]) * tiles[i]
                    mix = mix + (0.25 * cross[i, j]) * laps[i]
                f_out[j, at:end, z * N : (z + 1) * N] = (
                    tiles[j] + rate[j, z, at:end, :] * react + mix
                )

    side = jnp.zeros((N, N), f32)
    for s in range(4):
        for z in range(4):
            q = 4 * s + z
            side = jnp.where(j0 // 2 == q, pltpu.roll(state[s, z], 2 * q + 1, 1), side)
    side = side.T
    r8, c8 = iota((8, N), 0), iota((8, N), 1)
    has = 0.25 * jnp.where(r8 % 2 == 0, (l < ny - 1).astype(f32), (l > 0).astype(f32))
    has_x = 0.25 * (k > 0).astype(f32), 0.25 * (k < nx - 1).astype(f32)
    tails = [jnp.zeros((8, N), f32)] * 2
    for j in range(4):
        mix = cross[0, j] * side[0:8]
        for i in range(1, 4):
            mix = mix + cross[i, j] * side[8 * i : 8 * i + 8]
        mix = has * mix
        cols[j] = mix
        beside = []
        for p, row in enumerate((0, N - 1)):
            pieces = []
            for z in range(4):
                piece = cross[0, j] * state[0, z, row : row + 1, :]
                for i in range(1, 4):
                    piece = piece + cross[i, j] * state[i, z, row : row + 1, :]
                pieces.append(has_x[p] * piece)
            beside.append(jnp.concatenate(pieces, axis=1))
            by_plane(cells, p, j, beside[p])
        sums = dot_rows(hx[j], f_out[j])
        for p in range(2):
            c = hx[j, 2:3, 2 * p : 2 * p + 1], hx[j, 2:3, 2 * p + 1 : 2 * p + 2]
            by_plane(pay, p, j, sums[p : p + 1] + c[0] * beside[0] + c[1] * beside[1])
            total = jnp.sum(mix * hx[j, p : p + 1, :], axis=1, keepdims=True)
            tails[p] = jnp.where(c8 == j, total, tails[p])
    for p in range(2):
        pay[p, 16:24, :] = tails[p]
    for j in range(nx):
        send[j] = pay[(j < k).astype(jnp.int32)]


def rows_kernel(
    nx, ny, f_in, cells, cols, recv, wx, wx_cols, gx, lx, rx, hy, g_out, send, beside, pay
):
    l = lax.axis_index("col")
    incoming = dot_mixed(wx[...], recv[:, 0:16, :].reshape(nx * 16, N))
    from_before = incoming[0:16] + cells[0]
    from_after = incoming[16:32] + cells[1]
    in_cols = []
    for p in range(2):
        total = recv[0, 16:24, :] * wx_cols[p, 0:1, :]
        for j in range(1, nx):
            total = total + recv[j, 16:24, :] * wx_cols[p, j : j + 1, :]
        in_cols.append(total)
    for s in range(4):
        g = dot_rows(gx[s], f_in[s])
        lam, mu = lx[s, :, 0:1], lx[s, :, 1:2]
        col = (
            dot_rows(cols[s], gx[s], nt=True)
            + in_cols[0][:, s : s + 1] * rx[s, 0:1]
            + in_cols[1][:, s : s + 1] * rx[s, 1:2]
        )
        parts = []
        for z in range(4):
            q = slice(4 * s + z, 4 * s + z + 1)
            part = (
                g[:, z * N : (z + 1) * N] + lam * from_before[q] + mu * from_after[q]
            )
            g_out[s, z] = part
            parts.append(part)
        ends = dot_rows(hy[s], jnp.concatenate(parts, axis=0), nt=True)
        for p in range(2):
            c = hy[s, 2:3, 2 * p : 2 * p + 1], hy[s, 2:3, 2 * p + 1 : 2 * p + 2]
            for z in range(4):
                q = slice(4 * s + z, 4 * s + z + 1)
                after, before = col[2 * z : 2 * z + 1], col[2 * z + 1 : 2 * z + 2]
                pay[p, q, :] = (
                    ends[p : p + 1, z * N : (z + 1) * N] + c[0] * before + c[1] * after
                )
                beside[p, q, :] = after if p else before
    for m in range(ny):
        send[m] = pay[(m < l).astype(jnp.int32)]


def finish_cols(ny, g_in, recv, beside, wy, gy, ry, out, done=None):
    incoming = dot_mixed(wy[...], recv[...].reshape(ny * 16, N))
    lines = split(
        jnp.concatenate([incoming[0:16] + beside[0], incoming[16:32] + beside[1]], axis=0)
    )
    lines = jnp.concatenate(lines + lines, axis=0).T
    for s in range(4):
        res = dot_cols(g_in[s].reshape(4 * N, N), gy[s])
        outer = bdot(lines, ry[s])
        for z in range(4):
            at = slice(z * N, (z + 1) * N)
            out[s, z] = res[at] + outer[:, at]
        if done is not None:
            done(s)


def last_kernel(ny, g_in, recv, beside, wy, gy, ry, out, state, sent):
    copies = [
        pltpu.make_async_copy(state.at[s], out.at[s], sent.at[s]) for s in range(4)
    ]
    finish_cols(
        ny, g_in, recv, beside, wy, gy, ry, state, lambda s: copies[s].start()
    )
    for copy in copies:
        copy.wait()


def next_kernel(
    nx, ny, g_in, recv, beside, wy, gy, ry, rate, hx, kin, cross,
    f_out, send, cells, cols, state, pay,
):
    finish_cols(ny, g_in, recv, beside, wy, gy, ry, state)
    explicit(nx, ny, state, rate, hx, kin, cross, f_out, send, cells, cols, pay)


def call(body, outs, scratch, smem=0, place_out=pltpu.VMEM):
    shapes = [
        jax.ShapeDtypeStruct(shape, f32) if isinstance(shape, tuple) else shape
        for shape in outs
    ]

    def run(*args):
        count = len(args) - smem
        return pl.pallas_call(
            body,
            out_shape=shapes,
            in_specs=[pl.BlockSpec(memory_space=pltpu.VMEM)] * count
            + [pl.BlockSpec(memory_space=pltpu.SMEM)] * smem,
            out_specs=[pl.BlockSpec(memory_space=place_out)] * len(shapes),
            scratch_shapes=[
                pltpu.VMEM(shape, f32) if isinstance(shape, tuple) else shape
                for shape in scratch
            ],
            compiler_params=pltpu.CompilerParams(vmem_limit_bytes=VMEM),
            cost_estimate=pl.CostEstimate(
                flops=3_000_000_000, bytes_accessed=3_000_000, transcendentals=0
            ),
        )(*args)

    return run


def on_device(adjoint, rate_scale, kinetics, cross_matrix, x_diffusion, y_diffusion):
    nx, ny = lax.axis_size("row"), lax.axis_size("col")
    part = functools.partial
    weights = jax.ShapeDtypeStruct((4, N, 4 * N), bf16)
    gx, lx, rx, hx, gy, ry, hy, wx, wx_cols, wy = call(
        part(tables_kernel, nx, ny),
        [
            (4, N, N), (4, N, N), (4, 8, N), (4, 8, N), (4, N, N), weights, (4, 8, N),
            (32, nx * 16), (2, nx, N), (32, ny * 16),
        ],
        [(N, N)] * 8,
    )(1.0 / (M * jnp.concatenate([x_diffusion, y_diffusion], axis=1)))
    tile = (4, 4, N, N)
    step_out = [(4, N, 4 * N), (nx, 24, N), (2, 16, N), (4, 8, N)]
    f, send, cells, cols = call(part(explicit, nx, ny), step_out, [(2, 24, N)], 2)(
        adjoint, rate_scale, hx, kinetics, cross_matrix
    )
    for step in range(STEPS):
        recv = lax.all_to_all(send, "row", 0, 0, tiled=True)
        g, send, beside = call(
            part(rows_kernel, nx, ny), [tile, (ny, 16, N), (2, 16, N)], [(2, 16, N)]
        )(f, cells, cols, recv, wx, wx_cols, gx, lx, rx, hy)
        recv = lax.all_to_all(send, "col", 0, 0, tiled=True)
        if step + 1 < STEPS:
            f, send, cells, cols = call(
                part(next_kernel, nx, ny), step_out, [tile, (2, 24, N)], 2
            )(g, recv, beside, wy, gy, ry, rate_scale, hx, kinetics, cross_matrix)
    (out,) = call(
        part(last_kernel, ny),
        [tile],
        [tile, pltpu.SemaphoreType.DMA((4,))],
        place_out=pl.ANY,
    )(g, recv, beside, wy, gy, ry)
    return out


def solution(mesh):
    return jax.shard_map(
        on_device,
        mesh=mesh,
        in_specs=(P(None, None, "row", "col"), P(None, None, "row", "col"), P(), P(), P(), P()),
        out_specs=P(None, None, "row", "col"),
        check_vma=False,
    )
```

```python
import functools

import jax
import jax.numpy as jnp
from jax import lax
from jax.experimental import pallas as pl
from jax.experimental.pallas import tpu as pltpu
from jax.sharding import PartitionSpec as P

M = 1000.0
STEPS = 2
N = 128
STRIP = 32
f32 = jnp.float32
bf16 = jnp.bfloat16
VMEM = 20 * 1024 * 1024


def iota(shape, dim):
    return lax.broadcasted_iota(jnp.int32, shape, dim)


def split(a):
    hi = a.astype(bf16).astype(f32)
    return hi, a - hi


def bdot(a, b, nt=False):
    dims = (((1,), (1 if nt else 0,)), ((), ()))
    return lax.dot_general(
        a.astype(bf16), b.astype(bf16), dims, preferred_element_type=f32
    )


def dot_rows(a, b, nt=False):
    ah, al = split(a)
    bh, bl = split(b)
    n = a.shape[0]
    left = jnp.concatenate(
        [jnp.concatenate([ah, ah], axis=1), jnp.concatenate([al, al], axis=1)], axis=0
    )
    out = bdot(left, jnp.concatenate([bh, bl], axis=1 if nt else 0), nt)
    return out[0:n] + out[n:]


def dot_cols(a, b):
    ah, al = split(a)
    bh, bl = split(b)
    n = b.shape[1]
    right = jnp.concatenate([bh, bl], axis=1)
    out = bdot(
        jnp.concatenate([ah, al], axis=1), jnp.concatenate([right, right], axis=0)
    )
    return out[:, 0:n] + out[:, n:]


def dot_mixed(a, b):
    ah, al = split(a)
    bh, bl = split(b)
    m, n = a.shape[0], b.shape[1]
    out = bdot(jnp.concatenate([ah, al], axis=0), jnp.concatenate([bh, bl], axis=1))
    return (out[0:m, 0:n] + out[m:, n:]) + (out[0:m, n:] + out[m:, 0:n])


def pick(a, hit):
    hi, rest = split(a)
    mid, low = split(rest)
    n = a.shape[0]
    out = bdot(jnp.concatenate([hi, mid, low], axis=0), jnp.where(hit, 1.0, 0.0))
    return (out[0:n] + out[n : 2 * n]) + out[2 * n :]


def tables_kernel(
    nx, ny, eps_all, gx, lx, rx, hx, gy, ry, hy, wx, wy,
    rows_x, rows_y, ex, ey, p0, p1, q0, q1,
):
    k = lax.axis_index("row")
    l = lax.axis_index("col")
    rows_x[...] = jnp.full((N, N), 1.0 / M, f32)
    rows_y[...] = jnp.full((N, N), 1.0 / M, f32)
    for j in range(nx):
        rows_x[4 * j : 4 * j + 4, :] = eps_all[:, j * N : (j + 1) * N]
    for j in range(ny):
        rows_y[4 * j : 4 * j + 4, :] = eps_all[:, (nx + j) * N : (nx + j + 1) * N]

    def block(index):
        return eps_all[:, pl.ds(pl.multiple_of(index * N, N), N)]

    rows_y[32:36, :] = block(k)
    rows_y[36:40, :] = block(nx + l)
    ex[...] = rows_x[...].T
    ey[...] = rows_y[...].T

    first2 = (iota((2, N), 0) == 0).astype(f32)
    one, zero = jnp.ones((1, N), f32), jnp.zeros((1, N), f32)

    def advance(e, v, d):
        grown = e * v
        return (v + d) + grown, d + grown

    def body(i, carry):
        vx, dx, va, da, vb, db, ux, cx, ua, ca, ub, cb = carry
        at = pl.multiple_of(i * 8, 8)
        back = pl.multiple_of(N - 8 - i * 8, 8)
        ex_f, ey_f = ex[pl.ds(at, 8), :], ey[pl.ds(at, 8), :]
        ex_b, ey_b = ex[pl.ds(back, 8), :], ey[pl.ds(back, 8), :]
        for r in range(8):
            t = at + r
            p0[pl.ds(t, 1), :] = va
            p1[pl.ds(t, 1), :] = vb
            e, ee = ex_f[r : r + 1], ey_f[r : r + 1]
            vx, dx = advance(e, vx, dx)
            va, da = advance(ee, va, da)
            vb, db = advance(ee, vb, db)
            r2 = 7 - r
            t = back + r2
            q0[pl.ds(t, 1), :] = ua
            q1[pl.ds(t, 1), :] = ub
            e, ee = ex_b[r2 : r2 + 1], ey_b[r2 : r2 + 1]
            ux, cx = advance(e, ux, cx)
            ua, ca = advance(ee, ua, ca)
            ub, cb = advance(ee, ub, cb)
        return vx, dx, va, da, vb, db, ux, cx, ua, ca, ub, cb

    init = (first2, 1.0 - first2, one, zero, zero, one)
    vx, dx, va, da, vb, db, ux, cx, ua, ca, ub, cb = lax.fori_loop(
        0, N // 8, body, init + init
    )

    row = iota((8, N), 0)
    lane = iota((8, N), 1)
    blk = lane // 4
    forward = row < 2
    is_x = row % 2 == 0
    count = jnp.where(is_x, nx, ny)
    own = jnp.where(is_x, k, l)
    place = jnp.where(forward, blk, count - 1 - blk)
    own = jnp.where(forward, own, count - 1 - own)

    def pack(a, b, c, d):
        return jnp.where(
            row == 0, a, jnp.where(row == 1, b, jnp.where(row == 2, c, d))
        )

    def shifted(a, by):
        return jnp.where(
            forward, pltpu.roll(a, 4 * by, 1), pltpu.roll(a, N - 4 * by, 1)
        )

    def outside(by):
        return place < by

    a0 = pack(vx[0:1], va, ux[0:1], ua)
    b0 = pack(vx[1:2], vb, ux[1:2], ub)
    c0 = pack(dx[0:1], da, cx[0:1], ca)
    d0 = pack(dx[1:2], db, cx[1:2], cb)
    a, b, c, d = a0, b0, c0, d0
    by = 1
    while by < max(nx, ny):
        skip = outside(by)
        sa = jnp.where(skip, 1.0, shifted(a, by))
        sb = jnp.where(skip, 0.0, shifted(b, by))
        sc = jnp.where(skip, 0.0, shifted(c, by))
        sd = jnp.where(skip, 1.0, shifted(d, by))
        a, b, c, d = a * sa + b * sc, a * sb + b * sd, c * sa + d * sc, c * sb + d * sd
        by *= 2
        if by == 16:
            norm = 1.0 / (a + b)
            a, b, c, d = a * norm, b * norm, c * norm, d * norm
    skip = outside(1)
    slope = jnp.where(skip, 1.0, shifted((c + d) / (a + b), 1))

    decay = (1.0 - slope) / ((a0 + b0 * slope) - (c0 + d0 * slope))
    between = (place < own) & (place >= 0)
    prod = jnp.where(between, decay, 1.0)

    def against(a, by):
        return jnp.where(
            forward, pltpu.roll(a, N - 4 * by, 1), pltpu.roll(a, 4 * by, 1)
        )

    def past(by):
        return place + by >= count

    by = 1
    while by < max(nx, ny):
        prod = prod * jnp.where(past(by), 1.0, against(prod, by))
        by *= 2
    weight = jnp.where(between, jnp.where(past(1), 1.0, against(prod, 1)), 0.0)

    def expand(width, per_block, species_of):
        src = iota((N, width), 0)
        col = iota((N, width), 1)
        hit = (src // 4 == col // per_block) & (src % 4 == species_of(col % per_block))
        return pick(weight, hit)

    both = jnp.where(row < 4, weight[0:1], weight[2:3])
    wx[...] = jnp.where(lane % 4 == row % 4, both, 0.0)[:, 0 : nx * 4]
    width = ny * 16
    spread = expand(width, 16, lambda r: r // 4)
    rr, cc = iota((32, width), 0), iota((32, width), 1)
    wy[...] = jnp.where(
        rr % 16 == cc % 16, jnp.where(rr < 16, spread[1:2], spread[3:4]), 0.0
    )

    lane1 = iota((1, N), 1)
    to_x = lax.rem(32 - 4 * k + N, N)
    to_y = lax.rem(36 - 4 * l + N, N)
    sx = pltpu.roll(slope, to_x, 1)
    sy = pltpu.roll(slope, to_y, 1)
    valid = (lane1 >= 32) & (lane1 < 40)
    sf = jnp.where(valid, jnp.where(lane1 < 36, sx[0:1], sy[1:2]), 1.0)
    sb = jnp.where(valid, jnp.where(lane1 < 36, sx[2:3], sy[3:4]), 1.0)
    phi = p0[...] + p1[...] * sf
    psi = q0[...] + q1[...] * sb
    phi_before, phi_after = 1.0 - sf, va + vb * sf
    psi_after, psi_before = 1.0 - sb, ua + ub * sb
    wron = sf * psi_before + (ca + cb * sb) * phi_before
    inv_w = 1.0 / wron
    psi = psi * inv_w
    psi_after, psi_before = psi_after * inv_w, psi_before * inv_w
    phi_t, psi_t = phi.T, psi.T
    eps = ey[...]
    eps_t = rows_y[...]
    i0, j0 = iota((N, N), 0), iota((N, N), 1)
    low = i0 >= j0
    r8 = iota((8, N), 0)
    c8 = iota((8, N), 1)
    def from_either_end(pr, qr, ends):
        pb, pa, qb, qa = ends
        inv_p, inv_q = 1.0 / pr[:, N - 1 : N], 1.0 / qr[:, 0:1]
        beside = jnp.where(
            c8 == 0,
            pb * inv_p,
            jnp.where(c8 == 1, pa * inv_p, jnp.where(c8 == 2, qb * inv_q, qa * inv_q)),
        )
        return jnp.where(
            r8 == 0,
            pr * inv_p,
            jnp.where(r8 == 1, qr * inv_q, jnp.where(r8 == 2, beside, 0.0)),
        )

    wide = iota((N, 4 * N), 0)
    line, plane = wide % 16, iota((N, 4 * N), 1) // N
    from_after, high = (wide // 16) % 2 == 1, wide < 64

    for s in range(4):
        at = slice(32 + s, 33 + s)
        pr, qr, er = phi_t[at], psi_t[at], eps_t[at]
        pc, qc, ec = phi[:, at], psi[:, at], eps[:, at]
        ends = phi_before[:, at], phi_after[:, at], psi_before[:, at], psi_after[:, at]
        pb, pa, qb, qa = ends
        eq, ep = ec * qc, ec * pc
        gx[s] = jnp.where(low, eq * pr, ep * qr)
        lx[s] = jnp.where(j0 == 0, eq * pb, jnp.where(j0 == 1, ep * qa, 0.0))
        rx[s] = jnp.where(r8 == 0, pb * qr * er, jnp.where(r8 == 1, qa * pr * er, 0.0))
        hx[s] = from_either_end(pr, qr, ends)

        at = slice(36 + s, 37 + s)
        pr, qr, er = phi_t[at], psi_t[at], eps_t[at]
        pc, qc = phi[:, at], psi[:, at]
        ends = phi_before[:, at], phi_after[:, at], psi_before[:, at], psi_after[:, at]
        pb, pa, qb, qa = ends
        gy[s] = jnp.where(low, qc * (pr * er), pc * (qr * er))
        lam, mu = split(pb * qr * er), split(qa * pr * er)
        part = [
            jnp.where(from_after, jnp.concatenate([m] * 4, 1), jnp.concatenate([v] * 4, 1))
            for v, m in zip(lam, mu)
        ]
        ry[s] = jnp.where(
            line == 4 * s + plane, jnp.where(high, part[0], part[1]), 0.0
        ).astype(bf16)
        hy[s] = from_either_end(pr, qr, ends)


def by_plane(ref, p, s, values):
    for z in range(4):
        q = 4 * s + z
        ref[p, q : q + 1, :] = values[:, z * N : (z + 1) * N]


def explicit(nx, ny, state, rate, hx, kin, cross, f_out, send, cells, cols, pay):
    k, l = lax.axis_index("row"), lax.axis_index("col")
    j0 = iota((N, N), 1)
    ri, rj = iota((STRIP, N), 0), iota((STRIP, N), 1)
    for z in range(4):
        for at in range(0, N, STRIP):
            end = at + STRIP
            tiles, laps = [], []
            for s in range(4):
                t = state[s, z, at:end, :]
                if at == 0:
                    xm = jnp.where(ri == 0, 0.0, pltpu.roll(t, 1, 0))
                else:
                    xm = state[s, z, at - 1 : end - 1, :]
                if end == N:
                    xp = jnp.where(ri == STRIP - 1, 0.0, pltpu.roll(t, STRIP - 1, 0))
                else:
                    xp = state[s, z, at + 1 : end + 1, :]
                ym = jnp.where(rj == 0, 0.0, pltpu.roll(t, 1, 1))
                yp = jnp.where(rj == N - 1, 0.0, pltpu.roll(t, N - 1, 1))
                tiles.append(t)
                laps.append(xm + xp + ym + yp - 4.0 * t)
            for j in range(4):
                react = (0.5 * kin[0, j]) * tiles[0]
                mix = (0.25 * cross[0, j]) * laps[0]
                for i in range(1, 4):
                    react = react + (0.5 * kin[i, j]) * tiles[i]
                    mix = mix + (0.25 * cross[i, j]) * laps[i]
                f_out[j, at:end, z * N : (z + 1) * N] = (
                    tiles[j] + rate[j, z, at:end, :] * react + mix
                )

    side = jnp.zeros((N, N), f32)
    for s in range(4):
        for z in range(4):
            q = 4 * s + z
            side = jnp.where(j0 // 2 == q, pltpu.roll(state[s, z], 2 * q + 1, 1), side)
    side = side.T
    r8 = iota((8, N), 0)
    has = 0.25 * jnp.where(r8 % 2 == 0, (l < ny - 1).astype(f32), (l > 0).astype(f32))
    has_x = 0.25 * (k > 0).astype(f32), 0.25 * (k < nx - 1).astype(f32)
    pay[...] = jnp.zeros_like(pay)
    for j in range(4):
        mix = cross[0, j] * side[0:8]
        for i in range(1, 4):
            mix = mix + cross[i, j] * side[8 * i : 8 * i + 8]
        mix = has * mix
        cols[j] = mix
        beside = []
        for p, row in enumerate((0, N - 1)):
            pieces = []
            for z in range(4):
                piece = cross[0, j] * state[0, z, row : row + 1, :]
                for i in range(1, 4):
                    piece = piece + cross[i, j] * state[i, z, row : row + 1, :]
                pieces.append(has_x[p] * piece)
            beside.append(jnp.concatenate(pieces, axis=1))
            cells[p, j : j + 1, :] = beside[p]
        sums = dot_rows(hx[j], f_out[j])
        ends = dot_rows(hx[j], mix, nt=True)
        for p in range(2):
            c = hx[j, 2:3, 2 * p : 2 * p + 1], hx[j, 2:3, 2 * p + 1 : 2 * p + 2]
            pay[p, j : j + 1, 0 : 4 * N] = (
                sums[p : p + 1] + c[0] * beside[0] + c[1] * beside[1]
            )
            pay[p, j : j + 1, 4 * N : 4 * N + 8] = ends[p : p + 1]
    for j in range(nx):
        send[j] = pay[(j < k).astype(jnp.int32)]


def rows_kernel(
    nx, ny, f_in, cells, cols, recv, wx, gx, lx, rx, hy, g_out, send, beside, pay
):
    l = lax.axis_index("col")
    incoming = dot_rows(wx[...], recv[...].reshape(nx * 4, 5 * N))
    from_before = incoming[0:4, 0 : 4 * N] + cells[0]
    from_after = incoming[4:8, 0 : 4 * N] + cells[1]
    in_cols = jnp.concatenate(
        [incoming[:, 4 * N :], jnp.zeros((N - 8, N), f32)], axis=0
    ).T
    for s in range(4):
        g = dot_rows(gx[s], f_in[s])
        lam, mu = lx[s, :, 0:1], lx[s, :, 1:2]
        col = (
            dot_rows(cols[s], gx[s], nt=True)
            + in_cols[0:8, s : s + 1] * rx[s, 0:1]
            + in_cols[0:8, 4 + s : 5 + s] * rx[s, 1:2]
        )
        parts = []
        for z in range(4):
            at = slice(z * N, (z + 1) * N)
            part = (
                g[:, at] + lam * from_before[s : s + 1, at] + mu * from_after[s : s + 1, at]
            )
            g_out[s, z] = part
            parts.append(part)
        ends = dot_rows(hy[s], jnp.concatenate(parts, axis=0), nt=True)
        for p in range(2):
            c = hy[s, 2:3, 2 * p : 2 * p + 1], hy[s, 2:3, 2 * p + 1 : 2 * p + 2]
            for z in range(4):
                q = slice(4 * s + z, 4 * s + z + 1)
                after, before = col[2 * z : 2 * z + 1], col[2 * z + 1 : 2 * z + 2]
                pay[p, q, :] = (
                    ends[p : p + 1, z * N : (z + 1) * N] + c[0] * before + c[1] * after
                )
                beside[p, q, :] = after if p else before
    for m in range(ny):
        send[m] = pay[(m < l).astype(jnp.int32)]


def finish_cols(ny, g_in, recv, beside, wy, gy, ry, out, done=None):
    incoming = dot_mixed(wy[...], recv[...].reshape(ny * 16, N))
    lines = split(
        jnp.concatenate([incoming[0:16] + beside[0], incoming[16:32] + beside[1]], axis=0)
    )
    lines = jnp.concatenate(lines + lines, axis=0).T
    for s in range(4):
        res = dot_cols(g_in[s].reshape(4 * N, N), gy[s])
        outer = bdot(lines, ry[s])
        for z in range(4):
            at = slice(z * N, (z + 1) * N)
            out[s, z] = res[at] + outer[:, at]
        if done is not None:
            done(s)


def last_kernel(ny, g_in, recv, beside, wy, gy, ry, out, state, sent):
    copies = [
        pltpu.make_async_copy(state.at[s], out.at[s], sent.at[s]) for s in range(4)
    ]
    finish_cols(
        ny, g_in, recv, beside, wy, gy, ry, state, lambda s: copies[s].start()
    )
    for copy in copies:
        copy.wait()


def next_kernel(
    nx, ny, g_in, recv, beside, wy, gy, ry, rate, hx, kin, cross,
    f_out, send, cells, cols, state, pay,
):
    finish_cols(ny, g_in, recv, beside, wy, gy, ry, state)
    explicit(nx, ny, state, rate, hx, kin, cross, f_out, send, cells, cols, pay)


def call(body, outs, scratch, smem=0, place_out=pltpu.VMEM):
    shapes = [
        jax.ShapeDtypeStruct(shape, f32) if isinstance(shape, tuple) else shape
        for shape in outs
    ]

    def run(*args):
        count = len(args) - smem
        return pl.pallas_call(
            body,
            out_shape=shapes,
            in_specs=[pl.BlockSpec(memory_space=pltpu.VMEM)] * count
            + [pl.BlockSpec(memory_space=pltpu.SMEM)] * smem,
            out_specs=[pl.BlockSpec(memory_space=place_out)] * len(shapes),
            scratch_shapes=[
                pltpu.VMEM(shape, f32) if isinstance(shape, tuple) else shape
                for shape in scratch
            ],
            compiler_params=pltpu.CompilerParams(vmem_limit_bytes=VMEM),
            cost_estimate=pl.CostEstimate(
                flops=3_000_000_000, bytes_accessed=3_000_000, transcendentals=0
            ),
        )(*args)

    return run


def on_device(adjoint, rate_scale, kinetics, cross_matrix, x_diffusion, y_diffusion):
    nx, ny = lax.axis_size("row"), lax.axis_size("col")
    part = functools.partial
    weights = jax.ShapeDtypeStruct((4, N, 4 * N), bf16)
    gx, lx, rx, hx, gy, ry, hy, wx, wy = call(
        part(tables_kernel, nx, ny),
        [
            (4, N, N), (4, N, N), (4, 8, N), (4, 8, N), (4, N, N), weights, (4, 8, N),
            (8, nx * 4), (32, ny * 16),
        ],
        [(N, N)] * 8,
    )(1.0 / (M * jnp.concatenate([x_diffusion, y_diffusion], axis=1)))
    tile = (4, 4, N, N)
    step_out = [(4, N, 4 * N), (nx, 4, 5 * N), (2, 4, 4 * N), (4, 8, N)]
    f, send, cells, cols = call(part(explicit, nx, ny), step_out, [(2, 4, 5 * N)], 2)(
        adjoint, rate_scale, hx, kinetics, cross_matrix
    )
    for step in range(STEPS):
        recv = lax.all_to_all(send, "row", 0, 0, tiled=True)
        g, send, beside = call(
            part(rows_kernel, nx, ny), [tile, (ny, 16, N), (2, 16, N)], [(2, 16, N)]
        )(f, cells, cols, recv, wx, gx, lx, rx, hy)
        recv = lax.all_to_all(send, "col", 0, 0, tiled=True)
        if step + 1 < STEPS:
            f, send, cells, cols = call(
                part(next_kernel, nx, ny), step_out, [tile, (2, 4, 5 * N)], 2
            )(g, recv, beside, wy, gy, ry, rate_scale, hx, kinetics, cross_matrix)
    (out,) = call(
        part(last_kernel, ny),
        [tile],
        [tile, pltpu.SemaphoreType.DMA((4,))],
        place_out=pl.ANY,
    )(g, recv, beside, wy, gy, ry)
    return out


def solution(mesh):
    return jax.shard_map(
        on_device,
        mesh=mesh,
        in_specs=(P(None, None, "row", "col"), P(None, None, "row", "col"), P(), P(), P(), P()),
        out_specs=P(None, None, "row", "col"),
        check_vma=False,
    )
```
